512 devices in a mesh: tm: 32 (over z_lo, x, core), space: 16 (over z_hi, y).
Axes of the slice: x: 4, y: 4, z: 16 (z_hi: 4, z_lo: 4; z = z_hi * 4 + z_lo), core: 2. Of those that a mesh axis runs over, the one named last changes fastest.
Arguments:
- initial_state: float32 [768, 512], P('space'), may hold values from -6 to 6
- velocity: bfloat16 [768, 512], P('space'), may hold values from -0.5 to 0.5
- diffusion: bfloat16 [768, 512], P('space'), may hold values from 0.25 to 0.5
- forcing: bfloat16 [256, 768, 512], P('tm', 'space'), may hold values from -6 to 6
- implicit: float32 [512, 512], replicated, may hold values from 0 to 1
- coarse_implicit: float32 [512, 512], replicated, may hold values from 0 to 1
Outputs:
- solution: float32 [256, 768, 512], P('tm', 'space')
The draws below stay inside these ranges and needn't reach their ends.
All inputs are finite; a program needn't handle non-finite values.
Results may differ from the reference program's by a relative error of at most 0.0003.
Values may be sent and summed in bfloat16 or wider, within the bound.
A program may use at most 64 MiB of HBM per device.

```python
import math
import jax
import jax.numpy as jnp
from jax import lax

NY = 512
BLK = 8
CYCLES = 2
NX = 768
NT = 256
N_TM = 32


def implicit_matrix(key, lowest, highest):
    strengths = jnp.exp(jax.random.uniform(key, (NY,), jnp.float32, math.log(lowest), math.log(highest)))
    places = jnp.arange(NY)
    offsets = jnp.abs(places[:, None] - places[None, :])
    distance = jnp.minimum(offsets, NY - offsets).astype(jnp.float32)
    kernel = jnp.where(offsets == 0, 0.0, -1.0 / jnp.maximum(distance, 1.0) ** 1.5)
    identity = jnp.eye(NY, dtype=jnp.float32)
    kernel = kernel - identity * jnp.sum(kernel, axis=1)[:, None]
    system = identity + kernel * strengths[None, :]
    return jnp.clip(jnp.linalg.inv(system), 0.0, 1.0)


def draw_implicit(key, part):
    return implicit_matrix(jax.random.fold_in(key, 11), 0.05, 0.8)


def draw_coarse_implicit(key, part):
    return implicit_matrix(jax.random.fold_in(key, 23), 0.4, 6.4)


def draw_forcing(key, part):
    noise_part = jnp.clip(jax.random.normal(jax.random.fold_in(key, 5), (NT, NX, NY), jnp.float32), -6.0, 6.0)
    return noise_part.astype(jnp.bfloat16)


def level_of(stream_key, shape, split, least, largest):
    def one(axis_at, shards_of):
        heights = jax.random.uniform(jax.random.fold_in(jax.random.fold_in(stream_key, 6), axis_at), (shards_of,), jnp.float32, least / len(split), largest / len(split))
        return jnp.repeat(jnp.exp(heights), shape[axis_at] // shards_of).reshape((-1,) + (1,) * (len(shape) - axis_at - 1))

    gain = one(*split[0])
    for cut in split[1:]:
        gain = gain * one(*cut)
    return gain


def scatter_about(key, shape, scale, bound, cuts=(), held_as=jnp.bfloat16):
    gain = level_of(key, shape, cuts, -0.22, 0.18) if cuts else 1.0
    values = jax.random.normal(key, shape, jnp.float32) * scale * gain
    return jnp.minimum(jnp.maximum(values, -bound), bound).astype(held_as)


def setup_inputs(seed: int = 0) -> dict:
    streams_of = jax.random.split(jax.random.key(seed), 7)
    initial_state = scatter_about(streams_of[0], (NX, NY), 1.0, 6.0, ((0, 16),), jnp.float32)
    velocity = jnp.clip(jax.random.uniform(streams_of[1], (NX, NY), jnp.float32, -0.5, 0.5) * level_of(streams_of[1], (NX, NY), ((0, 16),), -0.4, 0.0), -0.5, 0.5).astype(jnp.bfloat16)
    diffusion = jnp.clip(0.25 + 0.25 * jax.random.uniform(streams_of[2], (NX, NY), jnp.float32) ** level_of(streams_of[2], (NX, NY), ((0, 16),), -0.2, 0.2), 0.25, 0.5).astype(jnp.bfloat16)
    forcing = draw_forcing(jax.random.fold_in(streams_of[6], 71), 0)
    implicit = draw_implicit(jax.random.fold_in(streams_of[6], 71), 0)
    coarse_implicit = draw_coarse_implicit(jax.random.fold_in(streams_of[6], 71), 0)
    return {"initial_state": initial_state, "velocity": velocity, "diffusion": diffusion, "forcing": forcing, "implicit": implicit, "coarse_implicit": coarse_implicit}


HIGHEST = lax.Precision.HIGHEST

def stencil_weights(velocity, diffusion):
    moving = velocity.astype(jnp.float32)
    spread = diffusion.astype(jnp.float32)
    return (spread + 0.5 * moving, 1.0 - 2.0 * spread, spread - 0.5 * moving)

def advance(current, forcing_now, weights, implicit):
    west_weight, centre_weight, east_weight = weights
    summed = centre_weight * current + east_weight * jnp.roll(current, -1, -2) + west_weight * jnp.roll(current, 1, -2) + forcing_now.astype(jnp.float32)
    return jnp.matmul(summed, implicit, precision=HIGHEST)

def sweep_blocks(starts, blocks, step_count, weights, implicit):
    current = starts
    values = []
    for offset in range(step_count):
        current = advance(current, blocks[:, offset], weights, implicit)
        values.append(current)
    return values

def reference(initial_state, velocity, diffusion, forcing, implicit, coarse_implicit):
    weights = stencil_weights(velocity, diffusion)
    blocks = forcing.reshape(N_TM, BLK, NX, NY)
    end_values = jnp.zeros((N_TM, NX, NY), jnp.float32)

    def coarse_chain(carried, residual):
        updated = jnp.matmul(carried, coarse_implicit, precision=HIGHEST) + residual
        return (updated, updated)
    for repeat in range(CYCLES):
        starts = jnp.concatenate([initial_state[None], end_values[:-1]], axis=0)
        end_values = sweep_blocks(starts, blocks, BLK, weights, implicit)[-1]
        starts = jnp.concatenate([initial_state[None], end_values[:-1]], axis=0)
        residual = sweep_blocks(starts, blocks, BLK, weights, implicit)[-1] - end_values
        _, errors = lax.scan(coarse_chain, jnp.zeros((NX, NY), jnp.float32), residual)
        end_values = end_values + errors
    starts = jnp.concatenate([initial_state[None], end_values[:-1]], axis=0)
    values = sweep_blocks(starts, blocks, BLK - 1, weights, implicit)
    return jnp.stack(values + [end_values], axis=1).reshape(NT, NX, NY)
```

```python
import functools

import jax
import jax.numpy as jnp
from jax import lax
from jax.experimental import pallas as pl
from jax.experimental.pallas import tpu as pltpu
from jax.sharding import PartitionSpec as P

F32, BF16 = jnp.float32, jnp.bfloat16
MESH = pl.DeviceIdType.MESH

STEPS = 8
NTM = 32
SLAB = 48
NY = 512
LANES = 128
GROUPS = NY // LANES
OWNERS = 12
ROWS = SLAB // OWNERS
TILE = ROWS * GROUPS
OUTER = 16
INNER = 8


def owner_of(chunk):
    return 8 + chunk + (2 if chunk >= OWNERS // 2 else 0)


def split(x):
    high = x.astype(BF16)
    return high, (x - high.astype(F32)).astype(BF16)


def dot(a, b):
    return jnp.dot(a, b, preferred_element_type=F32)


def dot3(x, high, low):
    rows = x.shape[0]
    xh, xl = split(x)
    both = dot(jnp.concatenate([xh, xl], axis=0), high)
    return both[:rows] + both[rows:] + dot(xh, low)


def kernel(u0_hbm, vel_hbm, dif_hbm, forcing_hbm, imp_hbm, coarse_hbm, out,
           mv, cv, mh, ml, cl, pw, plow, ptmp, fin, vin, din, uin, fpack, fhalo,
           wext, fext, bsend, brecv, dsend, drecv, flat, fwd_send, fwd_recv, flat2,
           back1_send, back1_recv, flat3, back2_send, back2_recv, chold,
           in_sem, halo_send, halo_recv, u_send, u_recv, sh_send, sh_recv,
           fs_sem, fr_sem, bks_sem, bkr_sem):
    p = lax.axis_index("tm")
    s = lax.axis_index("space")
    nsp = lax.axis_size("space")
    up = lax.rem(s + nsp - 1, nsp)
    down = lax.rem(s + 1, nsp)
    first = p == 0
    is_owner = ((p >= 8) & (p < 14)) | ((p >= 16) & (p < 22))
    chunk = jnp.where(p < 14, p - 8, p - 10)
    top_owner = is_owner & (chunk < 4)
    bottom_owner = is_owner & (chunk >= OWNERS - 4)
    top2_owner = is_owner & (chunk < 2)
    bottom2_owner = is_owner & (chunk >= OWNERS - 2)

    barrier = pltpu.get_barrier_semaphore()

    def greet(tm, space):
        pl.semaphore_signal(barrier, inc=1, device_id=(tm, space), device_id_type=MESH)

    greet(p, up)
    greet(p, down)

    @pl.when(p < NTM - 1)
    def _():
        for other in (up, s, down):
            greet(p + 1, other)

    @pl.when(p > 0)
    def _():
        for other in (up, s, down):
            greet(p - 1, other)

    for j in range(OWNERS):
        @pl.when(p != owner_of(j))
        def _():
            greet(owner_of(j), s)
        if j < 4:
            greet(owner_of(j), down)
        if j >= OWNERS - 4:
            greet(owner_of(j), up)

    @pl.when(is_owner)
    def _():
        @pl.loop(1, NTM)
        def _(i):
            greet(lax.rem(p + i, NTM), s)

    @pl.when(top_owner)
    def _():
        @pl.loop(0, NTM)
        def _(i):
            greet(i, up)

    @pl.when(bottom_owner)
    def _():
        @pl.loop(0, NTM)
        def _(i):
            greet(i, down)

    loads = [
        pltpu.make_async_copy(forcing_hbm, fin, in_sem.at[0]),
        pltpu.make_async_copy(imp_hbm, mv, in_sem.at[1]),
        pltpu.make_async_copy(vel_hbm, vin.at[pl.ds(OUTER, SLAB)], in_sem.at[2]),
        pltpu.make_async_copy(dif_hbm, din.at[pl.ds(OUTER, SLAB)], in_sem.at[3]),
        pltpu.make_async_copy(u0_hbm, uin.at[pl.ds(INNER, SLAB)], in_sem.at[4]),
        pltpu.make_async_copy(coarse_hbm, cv, in_sem.at[5]),
    ]
    for load in loads:
        load.start()

    loads[0].wait()
    sub = lax.broadcasted_iota(jnp.int32, (INNER, NY), 0)
    lower = [fin[k, SLAB - 16:SLAB, :].astype(F32)[8:] for k in range(7)]
    upper = [fin[k, 0:16, :].astype(F32)[:8] for k in range(7)]
    for side, rows in ((0, lower), (1, upper)):
        packed = []
        for k in range(4):
            if k == 3:
                packed.append(rows[3])
                continue
            count = k + 1
            if side == 0:
                moved = pltpu.roll(rows[6 - k], count, 0)
                packed.append(jnp.where(sub < count, moved, rows[k]))
            else:
                moved = pltpu.roll(rows[6 - k], INNER - count, 0)
                packed.append(jnp.where(sub >= INNER - count, moved, rows[k]))
        fpack[side] = jnp.concatenate(packed, axis=0).astype(BF16)

    total = (2 + 12 + 8 + jnp.where(p < NTM - 1, 3, 0) + jnp.where(p > 0, 3, 0)
             + jnp.where(is_owner, NTM - 2, 0)
             + jnp.where(top_owner, NTM, 0) + jnp.where(bottom_owner, NTM, 0))
    pl.semaphore_wait(barrier, total)

    def remote(src, dst, send, recv, tm, space):
        return pltpu.make_async_remote_copy(src_ref=src, dst_ref=dst, send_sem=send, recv_sem=recv,
                                            device_id=(tm, space), device_id_type=MESH)

    edge_low, edge_high = pl.ds(0, OUTER), pl.ds(OUTER + SLAB, OUTER)
    own_low, own_high = pl.ds(0, 16), pl.ds(SLAB - 16, 16)
    halos = [
        remote(fpack.at[0], fhalo.at[0], halo_send.at[0], halo_recv.at[0], p, down),
        remote(fpack.at[1], fhalo.at[1], halo_send.at[1], halo_recv.at[1], p, up),
        remote(vel_hbm.at[own_high], vin.at[edge_low], halo_send.at[2], halo_recv.at[2], p, down),
        remote(vel_hbm.at[own_low], vin.at[edge_high], halo_send.at[3], halo_recv.at[3], p, up),
        remote(dif_hbm.at[own_high], din.at[edge_low], halo_send.at[4], halo_recv.at[4], p, down),
        remote(dif_hbm.at[own_low], din.at[edge_high], halo_send.at[5], halo_recv.at[5], p, up),
    ]
    for copy in halos:
        copy.start()
    u_halos = [
        remote(u0_hbm.at[pl.ds(SLAB - INNER, INNER)], uin.at[pl.ds(0, INNER)], u_send.at[0], u_recv.at[0], p, down),
        remote(u0_hbm.at[pl.ds(0, INNER)], uin.at[pl.ds(INNER + SLAB, INNER)], u_send.at[1], u_recv.at[1], p, up),
    ]

    @pl.when(first)
    def _():
        for copy in u_halos:
            copy.start()

    loads[1].wait()
    a, b = split(mv[...])
    mh[...] = a
    ml[...] = b
    loads[5].wait()
    a, b = split(cv[...])
    pw[0] = a
    cl[...] = b
    plow[...] = b
    for k in range(STEPS):
        fext[k, INNER:INNER + SLAB, :] = fin[k].astype(F32)

    def square(k):
        @pl.loop(0, 4)
        def _(i):
            rows = pl.ds(pl.multiple_of(i * 128, 128), 128)
            xh, xl = pw[k - 1, rows, :], plow[rows, :]
            both = dot(jnp.concatenate([xh, xl], axis=0), pw[k - 1])
            ptmp[rows, :] = both[:128] + both[128:] + dot(xh, plow[...])

        high, low = split(ptmp[...])
        pw[k] = high
        plow[...] = low

    @pl.when(is_owner)
    def _():
        square(1)
        square(2)

    for load in loads[2:5]:
        load.wait()
    for copy in halos:
        copy.wait_recv()

    spread = din[...].astype(F32)
    half = 0.5 * vin[...].astype(F32)
    wext[0] = spread + half
    wext[1] = 1.0 - 2.0 * spread
    wext[2] = spread - half
    for side, at in ((0, 0), (1, INNER + SLAB)):
        packed = fhalo[side].astype(F32)
        for k in range(STEPS):
            if k < 4:
                rows = packed[8 * k:8 * k + 8]
            elif k < 7:
                rows = packed[8 * (6 - k):8 * (7 - k)]
                rows = pltpu.roll(rows, INNER - (7 - k) if side == 0 else 7 - k, 0)
            else:
                rows = jnp.zeros((INNER, NY), F32)
            fext[k, at:at + INNER, :] = rows

    @pl.when(first)
    def _():
        for copy in u_halos:
            copy.wait_recv()

    def advance(v, weights, forced):
        west, centre, east = weights
        rows = v.shape[0]
        mixed = centre * v + east * pltpu.roll(v, rows - 1, 0) + west * pltpu.roll(v, 1, 0)
        if forced is not None:
            mixed = mixed + forced
        return dot3(mixed, mh[...], ml[...])

    def weights64():
        return tuple(wext[i, 8:72, :] for i in range(3))

    def sweep(v, weights, forced):
        def turn(k, v):
            return advance(v, weights(), fext[k] if forced else None)
        return lax.fori_loop(0, STEPS, turn, v)

    def weights128():
        return tuple(jnp.concatenate([w, w], axis=0) for w in weights64())

    def weights80():
        return tuple(wext[i] for i in range(3))

    def shift(src, dst, at):
        return [
            remote(src, dst.at[pl.ds(INNER, SLAB)], sh_send.at[at], sh_recv.at[at], p + 1, s),
            remote(src.at[pl.ds(0, INNER)], dst.at[pl.ds(INNER + SLAB, INNER)],
                   sh_send.at[at + 1], sh_recv.at[at + 1], p + 1, up),
            remote(src.at[pl.ds(SLAB - INNER, INNER)], dst.at[pl.ds(0, INNER)],
                   sh_send.at[at + 2], sh_recv.at[at + 2], p + 1, down),
        ]

    def start_shift(copies):
        @pl.when(p < NTM - 1)
        def _():
            for copy in copies:
                copy.start()

    def end_shift(copies, dst):
        @pl.when(p > 0)
        def _():
            for copy in copies:
                copy.wait_recv()

        @pl.when(first)
        def _():
            dst[...] = jnp.zeros_like(dst)

    begin = jnp.where(first, uin[...], jnp.zeros((64, NY), F32))
    bsend[...] = sweep(begin, weights64, True)[8:56]
    b_copies = shift(bsend, brecv, 0)
    start_shift(b_copies)

    @pl.when(is_owner)
    def _():
        square(3)
        square(4)

    end_shift(b_copies, brecv)
    dsend[...] = sweep(brecv[...], weights64, False)[8:56]
    d_copies = shift(dsend, drecv, 3)

    def forward(which, rows):
        for g in range(GROUPS):
            flat[pl.ds(g, SLAB, stride=GROUPS), :] = rows[:, g * LANES:(g + 1) * LANES]
        fwd_send[which] = flat[...].astype(BF16)
        mine = pl.ds(pl.multiple_of(p * TILE, TILE), TILE)
        for j in range(OWNERS):
            part = pl.ds(j * TILE, TILE)
            copy = remote(fwd_send.at[which, part], fwd_recv.at[which, mine],
                          fs_sem.at[which], fr_sem.at[which], owner_of(j), s)

            @pl.when(p != owner_of(j))
            def _():
                copy.start()

            @pl.when(p == owner_of(j))
            def _():
                fwd_recv[which, mine, :] = fwd_send[which, part, :]

    def forward_end(which):
        def wait(n):
            remote(fwd_send.at[which, pl.ds(0, n * TILE)], fwd_recv.at[which, pl.ds(0, n * TILE)],
                   fs_sem.at[which], fr_sem.at[which], p, up).wait_send()

        @pl.when(is_owner)
        def _():
            wait(OWNERS - 1)

        @pl.when(jnp.logical_not(is_owner))
        def _():
            wait(OWNERS)

    def scan(which, delay, result):
        count = (NTM - 1) * TILE
        remote(fwd_recv.at[which, pl.ds(0, count)], fwd_recv.at[which, pl.ds(0, count)],
               fs_sem.at[which], fr_sem.at[which], p, up).wait_recv()
        flat2[...] = fwd_recv[which].astype(F32)
        size = NTM * ROWS
        total = jnp.concatenate([flat2[pl.ds(g, size, stride=GROUPS), :] for g in range(GROUPS)], axis=1)
        row = lax.broadcasted_iota(jnp.int32, (size, NY), 0)

        def later(x, blocks):
            return jnp.where(row >= blocks * ROWS, pltpu.roll(x, blocks * ROWS, 0), 0.0)

        total = later(total, delay)
        for k in range(5):
            total = total + dot(later(total, 1 << k).astype(BF16), pw[k])
        for g in range(GROUPS):
            flat2[pl.ds(g, size, stride=GROUPS), :] = total[:, g * LANES:(g + 1) * LANES]
        result[...] = flat2[...].astype(result.dtype)

    def back(which, src, dst, edge, top, bottom):
        def copy(block, place, space):
            return remote(src.at[pl.ds(pl.multiple_of(block * TILE, TILE), TILE)],
                          dst.at[pl.ds(pl.multiple_of(place * TILE, TILE), TILE)],
                          bks_sem.at[which], bkr_sem.at[which], block, space)

        @pl.when(top)
        def _():
            @pl.loop(0, NTM)
            def _(i):
                copy(i, edge + OWNERS + chunk, up).start()

        @pl.when(bottom)
        def _():
            @pl.loop(0, NTM)
            def _(i):
                copy(i, chunk - (OWNERS - edge), down).start()

        @pl.loop(1, NTM)
        def _(i):
            copy(lax.rem(p + i, NTM), edge + chunk, s).start()

        at = pl.ds(pl.multiple_of((edge + chunk) * TILE, TILE), TILE)
        dst[at, :] = src[pl.ds(pl.multiple_of(p * TILE, TILE), TILE), :]

    def back_wait(which, dst, edge):
        def wait(n):
            part = dst.at[pl.ds(0, n * TILE)]
            remote(part, part, bks_sem.at[which], bkr_sem.at[which], p, up).wait_recv()

        @pl.when(is_owner)
        def _():
            wait(OWNERS + 2 * edge - 1)

        @pl.when(jnp.logical_not(is_owner))
        def _():
            wait(OWNERS + 2 * edge)

    def back_end(which, src, on_edge):
        def wait(n):
            part = src.at[pl.ds(0, n * TILE)]
            remote(part, part, bks_sem.at[which], bkr_sem.at[which], p, up).wait_send()

        @pl.when(is_owner)
        def _():
            wait(NTM - 1)

        @pl.when(on_edge)
        def _():
            wait(NTM)

    forward(0, dsend[...])
    start_shift(d_copies)

    @pl.when(is_owner)
    def _():
        scan(0, 2, back1_send)
        back(0, back1_send, back1_recv, 4, top_owner, bottom_owner)

    back_wait(0, back1_recv, 4)
    flat3[...] = back1_recv[...].astype(F32)
    before = jnp.concatenate([flat3[pl.ds(g, 80, stride=GROUPS), :] for g in range(GROUPS)], axis=1)
    chold[...] = before

    previous_w = sweep(before, weights80, False)[8:72]
    end_shift(d_copies, drecv)
    carried = dot3(chold[8:72, :], pw[0], cl[...])
    pair = jnp.concatenate([previous_w - carried, drecv[...] + carried], axis=0)
    drecv[...] = brecv[...] + drecv[...] + previous_w
    pair = sweep(pair, weights128, False)
    residual = pair[8:56]
    forward(1, residual)
    out[7] = bsend[...] + dsend[...] + pair[72:120] + residual

    @pl.when(is_owner)
    def _():
        scan(1, 1, back2_send)
        back(1, back2_send, back2_recv, 2, top2_owner, bottom2_owner)

    back_wait(1, back2_recv, 2)
    correction = jnp.concatenate([back2_recv[pl.ds(g, 64, stride=GROUPS), :] for g in range(GROUPS)], axis=1)
    v = jnp.where(first, uin[...], drecv[...] + correction)
    out[7] = out[7] + dot3(correction[8:56], pw[0], cl[...])

    def last(k, v):
        v = advance(v, weights64(), fext[k])
        out[k] = v[8:56]
        return v

    lax.fori_loop(0, STEPS - 1, last, v)

    for sent in halos:
        sent.wait_send()

    @pl.when(first)
    def _():
        for sent in u_halos:
            sent.wait_send()

    @pl.when(p < NTM - 1)
    def _():
        for sent in b_copies + d_copies:
            sent.wait_send()

    forward_end(0)
    forward_end(1)
    back_end(0, back1_send, top_owner | bottom_owner)
    back_end(1, back2_send, top2_owner | bottom2_owner)


def per_device(initial_state, velocity, diffusion, forcing, implicit, coarse_implicit):
    V = pltpu.VMEM
    DMA = pltpu.SemaphoreType.DMA
    square = (NY, NY)
    scratch = [
        V(square, F32), V(square, F32), V(square, BF16), V(square, BF16), V(square, BF16),
        V((5,) + square, BF16), V(square, BF16), V(square, F32),
        V((STEPS, SLAB, NY), BF16), V((80, NY), BF16), V((80, NY), BF16), V((64, NY), F32),
        V((2, 32, NY), BF16), V((2, 32, NY), BF16),
        V((3, 80, NY), F32), V((STEPS, 64, NY), F32),
        V((SLAB, NY), F32), V((64, NY), F32), V((SLAB, NY), F32), V((64, NY), F32),
        V((SLAB * GROUPS, LANES), F32), V((2, SLAB * GROUPS, LANES), BF16),
        V((2, NTM * TILE, LANES), BF16), V((NTM * TILE, LANES), F32),
        V((NTM * TILE, LANES), BF16), V((80 * GROUPS, LANES), BF16), V((80 * GROUPS, LANES), F32),
        V((NTM * TILE, LANES), F32), V((64 * GROUPS, LANES), F32), V((80, NY), F32),
        DMA((6,)), DMA((6,)), DMA((6,)), DMA((2,)), DMA((2,)), DMA((6,)), DMA((6,)),
        DMA((2,)), DMA((2,)), DMA((2,)), DMA((2,)),
    ]
    return pl.pallas_call(
        kernel,
        out_shape=jax.ShapeDtypeStruct((STEPS, SLAB, NY), F32),
        in_specs=[pl.BlockSpec(memory_space=pl.ANY)] * 6,
        out_specs=pl.BlockSpec(memory_space=pltpu.VMEM),
        scratch_shapes=scratch,
        compiler_params=pltpu.CompilerParams(
            collective_id=0, has_side_effects=True, vmem_limit_bytes=40 * 2**20),
    )(initial_state, velocity, diffusion, forcing, implicit, coarse_implicit)


def solution(mesh):
    in_specs = (
        P("space", None),
        P("space", None),
        P("space", None),
        P("tm", "space", None),
        P(),
        P(),
    )
    return jax.shard_map(
        per_device, mesh=mesh, in_specs=in_specs, out_specs=P("tm", "space", None), check_vma=False
    )
```

```python
import functools

import jax
import jax.numpy as jnp
from jax import lax
from jax.experimental import pallas as pl
from jax.experimental.pallas import tpu as pltpu
from jax.sharding import PartitionSpec as P

F32, BF16 = jnp.float32, jnp.bfloat16
MESH = pl.DeviceIdType.MESH

STEPS = 8
NTM = 32
SLAB = 48
NY = 512
LANES = 128
GROUPS = NY // LANES
OWNERS = 12
ROWS = SLAB // OWNERS
TILE = ROWS * GROUPS
OUTER = 16
INNER = 8


OWNER_OF = (8, 10, 12, 14, 9, 13, 19, 23, 16, 18, 20, 22)


def owner_of(chunk):
    return OWNER_OF[chunk]


def split(x):
    high = x.astype(BF16)
    return high, (x - high.astype(F32)).astype(BF16)


def dot(a, b):
    return jnp.dot(a, b, preferred_element_type=F32)


def dot3(x, high, low):
    rows = x.shape[0]
    xh, xl = split(x)
    both = dot(jnp.concatenate([xh, xl], axis=0), high)
    return both[:rows] + both[rows:] + dot(xh, low)


def kernel(u0_hbm, vel_hbm, dif_hbm, forcing_hbm, imp_hbm, coarse_hbm, out,
           mv, cv, mh, ml, cl, pw, plow, ptmp, fin, vin, din, uin, fpack, fhalo,
           wext, fext, bsend, brecv, dsend, drecv, flat, fwd_send, fwd_recv, flat2,
           back1_send, back1_recv, flat3, back2_send, back2_recv, chold,
           in_sem, halo_send, halo_recv, u_send, u_recv, sh_send, sh_recv,
           fs_sem, fr_sem, bks_sem, bkr_sem):
    p = lax.axis_index("tm")
    s = lax.axis_index("space")
    nsp = lax.axis_size("space")
    up = lax.rem(s + nsp - 1, nsp)
    down = lax.rem(s + 1, nsp)
    first = p == 0
    chunk = jnp.int32(-1)
    for j in range(OWNERS):
        chunk = jnp.where(p == OWNER_OF[j], j, chunk)
    is_owner = chunk >= 0
    top_owner = is_owner & (chunk < 4)
    bottom_owner = is_owner & (chunk >= OWNERS - 4)
    top2_owner = is_owner & (chunk < 2)
    bottom2_owner = is_owner & (chunk >= OWNERS - 2)

    loads = [
        pltpu.make_async_copy(forcing_hbm, fin, in_sem.at[0]),
        pltpu.make_async_copy(imp_hbm, mv, in_sem.at[1]),
        pltpu.make_async_copy(vel_hbm, vin.at[pl.ds(OUTER, SLAB)], in_sem.at[2]),
        pltpu.make_async_copy(dif_hbm, din.at[pl.ds(OUTER, SLAB)], in_sem.at[3]),
        pltpu.make_async_copy(u0_hbm, uin.at[pl.ds(INNER, SLAB)], in_sem.at[4]),
        pltpu.make_async_copy(coarse_hbm, cv, in_sem.at[5]),
    ]
    for load in loads:
        load.start()

    barrier = pltpu.get_barrier_semaphore()

    def greet(tm, space):
        pl.semaphore_signal(barrier, inc=1, device_id=(tm, space), device_id_type=MESH)

    greet(p, up)
    greet(p, down)

    @pl.when(p < NTM - 1)
    def _():
        for other in (up, s, down):
            greet(p + 1, other)

    @pl.when(p > 0)
    def _():
        for other in (up, s, down):
            greet(p - 1, other)

    for j in range(OWNERS):
        @pl.when(p != owner_of(j))
        def _():
            greet(owner_of(j), s)
        if j < 4:
            greet(owner_of(j), down)
        if j >= OWNERS - 4:
            greet(owner_of(j), up)

    @pl.when(is_owner)
    def _():
        @pl.loop(1, NTM)
        def _(i):
            greet(lax.rem(p + i, NTM), s)

    @pl.when(top_owner)
    def _():
        @pl.loop(0, NTM)
        def _(i):
            greet(i, up)

    @pl.when(bottom_owner)
    def _():
        @pl.loop(0, NTM)
        def _(i):
            greet(i, down)

    total = (2 + 12 + 8 + jnp.where(p < NTM - 1, 3, 0) + jnp.where(p > 0, 3, 0)
             + jnp.where(is_owner, NTM - 2, 0)
             + jnp.where(top_owner, NTM, 0) + jnp.where(bottom_owner, NTM, 0))
    pl.semaphore_wait(barrier, total)

    def remote(src, dst, send, recv, tm, space):
        return pltpu.make_async_remote_copy(src_ref=src, dst_ref=dst, send_sem=send, recv_sem=recv,
                                            device_id=(tm, space), device_id_type=MESH)

    edge_low, edge_high = pl.ds(0, OUTER), pl.ds(OUTER + SLAB, OUTER)
    own_low, own_high = pl.ds(0, 16), pl.ds(SLAB - 16, 16)
    halos = [
        remote(fpack.at[0], fhalo.at[0], halo_send.at[0], halo_recv.at[0], p, down),
        remote(fpack.at[1], fhalo.at[1], halo_send.at[1], halo_recv.at[1], p, up),
        remote(vel_hbm.at[own_high], vin.at[edge_low], halo_send.at[2], halo_recv.at[2], p, down),
        remote(vel_hbm.at[own_low], vin.at[edge_high], halo_send.at[3], halo_recv.at[3], p, up),
        remote(dif_hbm.at[own_high], din.at[edge_low], halo_send.at[4], halo_recv.at[4], p, down),
        remote(dif_hbm.at[own_low], din.at[edge_high], halo_send.at[5], halo_recv.at[5], p, up),
    ]
    for copy in halos[2:]:
        copy.start()
    u_halos = [
        remote(u0_hbm.at[pl.ds(SLAB - INNER, INNER)], uin.at[pl.ds(0, INNER)], u_send.at[0], u_recv.at[0], p, down),
        remote(u0_hbm.at[pl.ds(0, INNER)], uin.at[pl.ds(INNER + SLAB, INNER)], u_send.at[1], u_recv.at[1], p, up),
    ]

    @pl.when(first)
    def _():
        for copy in u_halos:
            copy.start()

    loads[0].wait()
    sub = lax.broadcasted_iota(jnp.int32, (INNER, NY), 0)
    lower = [fin[k, SLAB - 16:SLAB, :].astype(F32)[8:] for k in range(7)]
    upper = [fin[k, 0:16, :].astype(F32)[:8] for k in range(7)]
    for side, rows in ((0, lower), (1, upper)):
        packed = []
        for k in range(4):
            if k == 3:
                packed.append(rows[3])
                continue
            count = k + 1
            if side == 0:
                moved = pltpu.roll(rows[6 - k], count, 0)
                packed.append(jnp.where(sub < count, moved, rows[k]))
            else:
                moved = pltpu.roll(rows[6 - k], INNER - count, 0)
                packed.append(jnp.where(sub >= INNER - count, moved, rows[k]))
        fpack[side] = jnp.concatenate(packed, axis=0).astype(BF16)

    for copy in halos[:2]:
        copy.start()

    loads[1].wait()
    a, b = split(mv[...])
    mh[...] = a
    ml[...] = b
    loads[5].wait()
    a, b = split(cv[...])
    pw[0] = a
    cl[...] = b
    plow[...] = b
    for k in range(STEPS):
        fext[k, INNER:INNER + SLAB, :] = fin[k].astype(F32)

    def square(k):
        @pl.loop(0, 4)
        def _(i):
            rows = pl.ds(pl.multiple_of(i * 128, 128), 128)
            xh, xl = pw[k - 1, rows, :], plow[rows, :]
            both = dot(jnp.concatenate([xh, xl], axis=0), pw[k - 1])
            ptmp[rows, :] = both[:128] + both[128:] + dot(xh, plow[...])

        high, low = split(ptmp[...])
        pw[k] = high
        plow[...] = low

    @pl.when(is_owner)
    def _():
        square(1)
        square(2)

    for load in loads[2:5]:
        load.wait()
    for copy in halos:
        copy.wait_recv()

    spread = din[...].astype(F32)
    half = 0.5 * vin[...].astype(F32)
    wext[0] = spread + half
    wext[1] = 1.0 - 2.0 * spread
    wext[2] = spread - half
    for side, at in ((0, 0), (1, INNER + SLAB)):
        packed = fhalo[side].astype(F32)
        for k in range(STEPS):
            if k < 4:
                rows = packed[8 * k:8 * k + 8]
            elif k < 7:
                rows = packed[8 * (6 - k):8 * (7 - k)]
                rows = pltpu.roll(rows, INNER - (7 - k) if side == 0 else 7 - k, 0)
            else:
                rows = jnp.zeros((INNER, NY), F32)
            fext[k, at:at + INNER, :] = rows

    @pl.when(first)
    def _():
        for copy in u_halos:
            copy.wait_recv()

    def advance(v, weights, forced):
        west, centre, east = weights
        rows = v.shape[0]
        mixed = centre * v + east * pltpu.roll(v, rows - 1, 0) + west * pltpu.roll(v, 1, 0)
        if forced is not None:
            mixed = mixed + forced
        return dot3(mixed, mh[...], ml[...])

    def weights64():
        return tuple(wext[i, 8:72, :] for i in range(3))

    def sweep(v, weights, forced):
        def turn(k, v):
            return advance(v, weights(), fext[k] if forced else None)
        return lax.fori_loop(0, STEPS, turn, v)

    def weights128():
        return tuple(jnp.concatenate([w, w], axis=0) for w in weights64())

    def weights80():
        return tuple(wext[i] for i in range(3))

    def shift(src, dst, at):
        return [
            remote(src, dst.at[pl.ds(INNER, SLAB)], sh_send.at[at], sh_recv.at[at], p + 1, s),
            remote(src.at[pl.ds(0, INNER)], dst.at[pl.ds(INNER + SLAB, INNER)],
                   sh_send.at[at + 1], sh_recv.at[at + 1], p + 1, up),
            remote(src.at[pl.ds(SLAB - INNER, INNER)], dst.at[pl.ds(0, INNER)],
                   sh_send.at[at + 2], sh_recv.at[at + 2], p + 1, down),
        ]

    def start_shift(copies):
        @pl.when(p < NTM - 1)
        def _():
            for copy in copies:
                copy.start()

    def end_shift(copies, dst):
        @pl.when(p > 0)
        def _():
            for copy in copies:
                copy.wait_recv()

        @pl.when(first)
        def _():
            dst[...] = jnp.zeros_like(dst)

    begin = jnp.where(first, uin[...], jnp.zeros((64, NY), F32))
    bsend[...] = sweep(begin, weights64, True)[8:56]
    b_copies = shift(bsend, brecv, 0)
    start_shift(b_copies)

    @pl.when(is_owner)
    def _():
        square(3)
        square(4)

    end_shift(b_copies, brecv)
    dsend[...] = sweep(brecv[...], weights64, False)[8:56]
    d_copies = shift(dsend, drecv, 3)

    def forward(which, rows):
        for g in range(GROUPS):
            flat[pl.ds(g, SLAB, stride=GROUPS), :] = rows[:, g * LANES:(g + 1) * LANES]
        fwd_send[which] = flat[...].astype(BF16)
        mine = pl.ds(pl.multiple_of(p * TILE, TILE), TILE)
        for j in range(OWNERS):
            part = pl.ds(j * TILE, TILE)
            copy = remote(fwd_send.at[which, part], fwd_recv.at[which, mine],
                          fs_sem.at[which], fr_sem.at[which], owner_of(j), s)

            @pl.when(p != owner_of(j))
            def _():
                copy.start()

            @pl.when(p == owner_of(j))
            def _():
                fwd_recv[which, mine, :] = fwd_send[which, part, :]

    def forward_end(which):
        def wait(n):
            remote(fwd_send.at[which, pl.ds(0, n * TILE)], fwd_recv.at[which, pl.ds(0, n * TILE)],
                   fs_sem.at[which], fr_sem.at[which], p, up).wait_send()

        @pl.when(is_owner)
        def _():
            wait(OWNERS - 1)

        @pl.when(jnp.logical_not(is_owner))
        def _():
            wait(OWNERS)

    def scan(which, delay, result):
        count = (NTM - 1) * TILE
        remote(fwd_recv.at[which, pl.ds(0, count)], fwd_recv.at[which, pl.ds(0, count)],
               fs_sem.at[which], fr_sem.at[which], p, up).wait_recv()
        flat2[...] = fwd_recv[which].astype(F32)
        size = NTM * ROWS
        total = jnp.concatenate([flat2[pl.ds(g, size, stride=GROUPS), :] for g in range(GROUPS)], axis=1)
        row = lax.broadcasted_iota(jnp.int32, (size, NY), 0)

        def later(x, blocks):
            return jnp.where(row >= blocks * ROWS, pltpu.roll(x, blocks * ROWS, 0), 0.0)

        total = later(total, delay)
        for k in range(5):
            total = total + dot(later(total, 1 << k).astype(BF16), pw[k])
        for g in range(GROUPS):
            flat2[pl.ds(g, size, stride=GROUPS), :] = total[:, g * LANES:(g + 1) * LANES]
        result[...] = flat2[...].astype(result.dtype)

    def back(which, src, dst, edge, top, bottom):
        def copy(block, place, space):
            return remote(src.at[pl.ds(pl.multiple_of(block * TILE, TILE), TILE)],
                          dst.at[pl.ds(pl.multiple_of(place * TILE, TILE), TILE)],
                          bks_sem.at[which], bkr_sem.at[which], block, space)

        @pl.when(top)
        def _():
            @pl.loop(0, NTM)
            def _(i):
                copy(i, edge + OWNERS + chunk, up).start()

        @pl.when(bottom)
        def _():
            @pl.loop(0, NTM)
            def _(i):
                copy(i, chunk - (OWNERS - edge), down).start()

        @pl.loop(1, NTM)
        def _(i):
            copy(lax.rem(p + i, NTM), edge + chunk, s).start()

        at = pl.ds(pl.multiple_of((edge + chunk) * TILE, TILE), TILE)
        dst[at, :] = src[pl.ds(pl.multiple_of(p * TILE, TILE), TILE), :]

    def back_wait(which, dst, edge):
        def wait(n):
            part = dst.at[pl.ds(0, n * TILE)]
            remote(part, part, bks_sem.at[which], bkr_sem.at[which], p, up).wait_recv()

        @pl.when(is_owner)
        def _():
            wait(OWNERS + 2 * edge - 1)

        @pl.when(jnp.logical_not(is_owner))
        def _():
            wait(OWNERS + 2 * edge)

    def back_end(which, src, on_edge):
        def wait(n):
            part = src.at[pl.ds(0, n * TILE)]
            remote(part, part, bks_sem.at[which], bkr_sem.at[which], p, up).wait_send()

        @pl.when(is_owner)
        def _():
            wait(NTM - 1)

        @pl.when(on_edge)
        def _():
            wait(NTM)

    forward(0, dsend[...])
    start_shift(d_copies)

    @pl.when(is_owner)
    def _():
        scan(0, 2, back1_send)
        back(0, back1_send, back1_recv, 4, top_owner, bottom_owner)

    back_wait(0, back1_recv, 4)
    flat3[...] = back1_recv[...].astype(F32)
    before = jnp.concatenate([flat3[pl.ds(g, 80, stride=GROUPS), :] for g in range(GROUPS)], axis=1)
    chold[...] = before

    previous_w = sweep(before, weights80, False)[8:72]
    end_shift(d_copies, drecv)
    carried = dot3(chold[8:72, :], pw[0], cl[...])
    pair = jnp.concatenate([previous_w - carried, drecv[...] + carried], axis=0)
    drecv[...] = brecv[...] + drecv[...] + previous_w
    pair = sweep(pair, weights128, False)
    residual = pair[8:56]
    forward(1, residual)
    out[7] = bsend[...] + dsend[...] + pair[72:120] + residual

    @pl.when(is_owner)
    def _():
        scan(1, 1, back2_send)
        back(1, back2_send, back2_recv, 2, top2_owner, bottom2_owner)

    back_wait(1, back2_recv, 2)
    correction = jnp.concatenate([back2_recv[pl.ds(g, 64, stride=GROUPS), :] for g in range(GROUPS)], axis=1)
    v = jnp.where(first, uin[...], drecv[...] + correction)
    out[7] = out[7] + dot3(correction[8:56], pw[0], cl[...])

    def last(k, v):
        v = advance(v, weights64(), fext[k])
        out[k] = v[8:56]
        return v

    lax.fori_loop(0, STEPS - 1, last, v)

    for sent in halos:
        sent.wait_send()

    @pl.when(first)
    def _():
        for sent in u_halos:
            sent.wait_send()

    @pl.when(p < NTM - 1)
    def _():
        for sent in b_copies + d_copies:
            sent.wait_send()

    forward_end(0)
    forward_end(1)
    back_end(0, back1_send, top_owner | bottom_owner)
    back_end(1, back2_send, top2_owner | bottom2_owner)


def per_device(initial_state, velocity, diffusion, forcing, implicit, coarse_implicit):
    V = pltpu.VMEM
    DMA = pltpu.SemaphoreType.DMA
    square = (NY, NY)
    scratch = [
        V(square, F32), V(square, F32), V(square, BF16), V(square, BF16), V(square, BF16),
        V((5,) + square, BF16), V(square, BF16), V(square, F32),
        V((STEPS, SLAB, NY), BF16), V((80, NY), BF16), V((80, NY), BF16), V((64, NY), F32),
        V((2, 32, NY), BF16), V((2, 32, NY), BF16),
        V((3, 80, NY), F32), V((STEPS, 64, NY), F32),
        V((SLAB, NY), F32), V((64, NY), F32), V((SLAB, NY), F32), V((64, NY), F32),
        V((SLAB * GROUPS, LANES), F32), V((2, SLAB * GROUPS, LANES), BF16),
        V((2, NTM * TILE, LANES), BF16), V((NTM * TILE, LANES), F32),
        V((NTM * TILE, LANES), BF16), V((80 * GROUPS, LANES), BF16), V((80 * GROUPS, LANES), F32),
        V((NTM * TILE, LANES), F32), V((64 * GROUPS, LANES), F32), V((80, NY), F32),
        DMA((6,)), DMA((6,)), DMA((6,)), DMA((2,)), DMA((2,)), DMA((6,)), DMA((6,)),
        DMA((2,)), DMA((2,)), DMA((2,)), DMA((2,)),
    ]
    return pl.pallas_call(
        kernel,
        out_shape=jax.ShapeDtypeStruct((STEPS, SLAB, NY), F32),
        in_specs=[pl.BlockSpec(memory_space=pl.ANY)] * 6,
        out_specs=pl.BlockSpec(memory_space=pltpu.VMEM),
        scratch_shapes=scratch,
        compiler_params=pltpu.CompilerParams(
            collective_id=0, has_side_effects=True, vmem_limit_bytes=40 * 2**20),
    )(*[pltpu.with_memory_space_constraint(x, pltpu.HBM)
        for x in (initial_state, velocity, diffusion, forcing, implicit, coarse_implicit)])


def solution(mesh):
    in_specs = (
        P("space", None),
        P("space", None),
        P("space", None),
        P("tm", "space", None),
        P(),
        P(),
    )
    return jax.shard_map(
        per_device, mesh=mesh, in_specs=in_specs, out_specs=P("tm", "space", None), check_vma=False
    )
```

```python
import functools

import jax
import jax.numpy as jnp
from jax import lax
from jax.experimental import pallas as pl
from jax.experimental.pallas import tpu as pltpu
from jax.sharding import PartitionSpec as P

F32, BF16 = jnp.float32, jnp.bfloat16
MESH = pl.DeviceIdType.MESH

STEPS = 8
NTM = 32
SLAB = 48
NY = 512
LANES = 128
GROUPS = NY // LANES
OWNERS = 12
ROWS = SLAB // OWNERS
TILE = ROWS * GROUPS
OUTER = 16
INNER = 8


OWNER_OF = (8, 10, 12, 14, 9, 13, 19, 23, 16, 18, 20, 22)


def owner_of(chunk):
    return OWNER_OF[chunk]


def split(x):
    high = x.astype(BF16)
    return high, (x - high.astype(F32)).astype(BF16)


def dot(a, b):
    return jnp.dot(a, b, preferred_element_type=F32)


def dot3(x, high, low):
    rows = x.shape[0]
    xh, xl = split(x)
    both = dot(jnp.concatenate([xh, xl], axis=0), high)
    return both[:rows] + both[rows:] + dot(xh, low)


def kernel(u0_hbm, vel_hbm, dif_hbm, forcing_hbm, imp_hbm, coarse_hbm, out,
           mv, cv, mh, ml, cl, pw, plow, ptmp, fin, vin, din, uin, fpack, fhalo,
           wext, fext, fprev, bsend, brecv, dsend, drecv, flat, fwd_send, fwd_recv, flat2,
           back1_send, back1_recv, flat3, back2_send, back2_recv, chold, carry,
           in_sem, halo_send, halo_recv, u_send, u_recv, sh_send, sh_recv,
           fs_sem, fr_sem, bks_sem, bkr_sem):
    p = lax.axis_index("tm")
    s = lax.axis_index("space")
    nsp = lax.axis_size("space")
    up = lax.rem(s + nsp - 1, nsp)
    down = lax.rem(s + 1, nsp)
    first = p == 0
    starts = p < 2
    chunk = jnp.int32(-1)
    for j in range(OWNERS):
        chunk = jnp.where(p == OWNER_OF[j], j, chunk)
    is_owner = chunk >= 0
    top_owner = is_owner & (chunk < 4)
    bottom_owner = is_owner & (chunk >= OWNERS - 4)
    top2_owner = is_owner & (chunk < 2)
    bottom2_owner = is_owner & (chunk >= OWNERS - 2)

    loads = [
        pltpu.make_async_copy(forcing_hbm, fin, in_sem.at[0]),
        pltpu.make_async_copy(imp_hbm, mv, in_sem.at[1]),
        pltpu.make_async_copy(vel_hbm, vin.at[pl.ds(OUTER, SLAB)], in_sem.at[2]),
        pltpu.make_async_copy(dif_hbm, din.at[pl.ds(OUTER, SLAB)], in_sem.at[3]),
        pltpu.make_async_copy(u0_hbm, uin.at[pl.ds(OUTER, SLAB)], in_sem.at[4]),
        pltpu.make_async_copy(coarse_hbm, cv, in_sem.at[5]),
    ]
    for load in loads:
        load.start()

    barrier = pltpu.get_barrier_semaphore()

    def greet(tm, space):
        pl.semaphore_signal(barrier, inc=1, device_id=(tm, space), device_id_type=MESH)

    greet(p, up)
    greet(p, down)

    @pl.when(p < NTM - 1)
    def _():
        for other in (up, s, down):
            greet(p + 1, other)

    @pl.when(p > 0)
    def _():
        for other in (up, s, down):
            greet(p - 1, other)

    for j in range(OWNERS):
        @pl.when(p != owner_of(j))
        def _():
            greet(owner_of(j), s)
        if j < 4:
            greet(owner_of(j), down)
        if j >= OWNERS - 4:
            greet(owner_of(j), up)

    @pl.when(is_owner)
    def _():
        @pl.loop(1, NTM)
        def _(i):
            greet(lax.rem(p + i, NTM), s)

    @pl.when(top_owner)
    def _():
        @pl.loop(0, NTM)
        def _(i):
            greet(i, up)

    @pl.when(bottom_owner)
    def _():
        @pl.loop(0, NTM)
        def _(i):
            greet(i, down)

    total = (2 + 12 + 8 + jnp.where(p < NTM - 1, 3, 0) + jnp.where(p > 0, 3, 0)
             + jnp.where(is_owner, NTM - 2, 0)
             + jnp.where(top_owner, NTM, 0) + jnp.where(bottom_owner, NTM, 0))
    pl.semaphore_wait(barrier, total)

    def remote(src, dst, send, recv, tm, space):
        return pltpu.make_async_remote_copy(src_ref=src, dst_ref=dst, send_sem=send, recv_sem=recv,
                                            device_id=(tm, space), device_id_type=MESH)

    edge_low, edge_high = pl.ds(0, OUTER), pl.ds(OUTER + SLAB, OUTER)
    own_low, own_high = pl.ds(0, 16), pl.ds(SLAB - 16, 16)
    halos = [
        remote(fpack.at[0], fhalo.at[0], halo_send.at[0], halo_recv.at[0], p, down),
        remote(fpack.at[1], fhalo.at[1], halo_send.at[1], halo_recv.at[1], p, up),
        remote(vel_hbm.at[own_high], vin.at[edge_low], halo_send.at[2], halo_recv.at[2], p, down),
        remote(vel_hbm.at[own_low], vin.at[edge_high], halo_send.at[3], halo_recv.at[3], p, up),
        remote(dif_hbm.at[own_high], din.at[edge_low], halo_send.at[4], halo_recv.at[4], p, down),
        remote(dif_hbm.at[own_low], din.at[edge_high], halo_send.at[5], halo_recv.at[5], p, up),
    ]
    u_halos = [
        remote(u0_hbm.at[own_high], uin.at[edge_low], u_send.at[0], u_recv.at[0], p, down),
        remote(u0_hbm.at[own_low], uin.at[edge_high], u_send.at[1], u_recv.at[1], p, up),
    ]

    half_steps = STEPS // 2
    ahead = []
    for at in range(2):
        steps = pl.ds(at * half_steps, half_steps)
        ahead += [
            remote(forcing_hbm.at[steps, own_low], fprev.at[steps, edge_high],
                   sh_send.at[3 * at], sh_recv.at[3 * at], p + 1, up),
            remote(forcing_hbm.at[steps, own_high], fprev.at[steps, edge_low],
                   sh_send.at[3 * at + 1], sh_recv.at[3 * at + 1], p + 1, down),
            remote(forcing_hbm.at[steps], fprev.at[steps, pl.ds(OUTER, SLAB)],
                   sh_send.at[3 * at + 2], sh_recv.at[3 * at + 2], p + 1, s),
        ]

    for copy in halos[2:]:
        copy.start()

    @pl.when(starts)
    def _():
        for copy in u_halos:
            copy.start()

    @pl.when(p < NTM - 1)
    def _():
        for copy in ahead:
            copy.start()

    @pl.when(first)
    def _():
        fprev[...] = jnp.zeros_like(fprev)

    loads[0].wait()
    sub = lax.broadcasted_iota(jnp.int32, (INNER, NY), 0)
    lower = [fin[k, SLAB - 16:SLAB, :].astype(F32)[8:] for k in range(7)]
    upper = [fin[k, 0:16, :].astype(F32)[:8] for k in range(7)]
    for side, rows in ((0, lower), (1, upper)):
        packed = []
        for k in range(4):
            if k == 3:
                packed.append(rows[3])
                continue
            count = k + 1
            if side == 0:
                moved = pltpu.roll(rows[6 - k], count, 0)
                packed.append(jnp.where(sub < count, moved, rows[k]))
            else:
                moved = pltpu.roll(rows[6 - k], INNER - count, 0)
                packed.append(jnp.where(sub >= INNER - count, moved, rows[k]))
        fpack[side] = jnp.concatenate(packed, axis=0).astype(BF16)

    for copy in halos[:2]:
        copy.start()

    loads[1].wait()
    a, b = split(mv[...])
    mh[...] = a
    ml[...] = b
    loads[5].wait()
    a, b = split(cv[...])
    pw[0] = a
    cl[...] = b
    plow[...] = b
    for k in range(STEPS):
        fext[k, INNER:INNER + SLAB, :] = fin[k].astype(F32)

    def square(k):
        @pl.loop(0, 4)
        def _(i):
            rows = pl.ds(pl.multiple_of(i * 128, 128), 128)
            xh, xl = pw[k - 1, rows, :], plow[rows, :]
            both = dot(jnp.concatenate([xh, xl], axis=0), pw[k - 1])
            ptmp[rows, :] = both[:128] + both[128:] + dot(xh, plow[...])

        high, low = split(ptmp[...])
        pw[k] = high
        plow[...] = low

    @pl.when(is_owner)
    def _():
        for k in range(1, 5):
            square(k)

    for load in loads[2:5]:
        load.wait()
    for copy in halos[2:]:
        copy.wait_recv()

    spread = din[...].astype(F32)
    half = 0.5 * vin[...].astype(F32)
    wext[0] = spread + half
    wext[1] = 1.0 - 2.0 * spread
    wext[2] = spread - half
    @pl.when(starts)
    def _():
        for copy in u_halos:
            copy.wait_recv()

    def advance(v, weights, forced):
        west, centre, east = weights
        rows = v.shape[0]
        mixed = centre * v + east * pltpu.roll(v, rows - 1, 0) + west * pltpu.roll(v, 1, 0)
        if forced is not None:
            mixed = mixed + forced
        return dot3(mixed, mh[...], ml[...])

    def weights64():
        return tuple(wext[i, 8:72, :] for i in range(3))

    def sweep(v, weights, forced):
        def turn(k, v):
            return advance(v, weights(), fext[k] if forced else None)
        return lax.fori_loop(0, STEPS, turn, v)

    def weights128():
        return tuple(jnp.concatenate([w, w], axis=0) for w in weights64())

    def weights80():
        return tuple(wext[i] for i in range(3))

    def shift(src, dst, at):
        return [
            remote(src, dst.at[pl.ds(INNER, SLAB)], sh_send.at[at], sh_recv.at[at], p + 1, s),
            remote(src.at[pl.ds(0, INNER)], dst.at[pl.ds(INNER + SLAB, INNER)],
                   sh_send.at[at + 1], sh_recv.at[at + 1], p + 1, up),
            remote(src.at[pl.ds(SLAB - INNER, INNER)], dst.at[pl.ds(0, INNER)],
                   sh_send.at[at + 2], sh_recv.at[at + 2], p + 1, down),
        ]

    def start_shift(copies):
        @pl.when(p < NTM - 1)
        def _():
            for copy in copies:
                copy.start()

    def end_shift(copies, dst):
        @pl.when(p > 0)
        def _():
            for copy in copies:
                copy.wait_recv()

        @pl.when(first)
        def _():
            dst[...] = jnp.zeros_like(dst)

    def arrive(copies):
        @pl.when(p > 0)
        def _():
            for copy in copies:
                copy.wait_recv()

    def turn_before(k, v):
        return advance(v, weights80(), fprev[k].astype(F32))

    arrive(ahead[:3])
    v = jnp.where(p == 1, uin[...], jnp.zeros((80, NY), F32))
    v = lax.fori_loop(0, half_steps, turn_before, v)
    chold[...] = v
    arrive(ahead[3:])
    v = lax.fori_loop(half_steps, STEPS, turn_before, chold[...])
    brecv[...] = v[8:72]
    dsend[...] = sweep(v[8:72], weights64, False)[8:56]
    d_copies = shift(dsend, drecv, 6)

    def forward(which, rows):
        for g in range(GROUPS):
            flat[pl.ds(g, SLAB, stride=GROUPS), :] = rows[:, g * LANES:(g + 1) * LANES]
        fwd_send[which] = flat[...].astype(BF16)
        mine = pl.ds(pl.multiple_of(p * TILE, TILE), TILE)
        for j in range(OWNERS):
            part = pl.ds(j * TILE, TILE)
            copy = remote(fwd_send.at[which, part], fwd_recv.at[which, mine],
                          fs_sem.at[which], fr_sem.at[which], owner_of(j), s)

            @pl.when(p != owner_of(j))
            def _():
                copy.start()

            @pl.when(p == owner_of(j))
            def _():
                fwd_recv[which, mine, :] = fwd_send[which, part, :]

    def forward_end(which):
        def wait(n):
            remote(fwd_send.at[which, pl.ds(0, n * TILE)], fwd_recv.at[which, pl.ds(0, n * TILE)],
                   fs_sem.at[which], fr_sem.at[which], p, up).wait_send()

        @pl.when(is_owner)
        def _():
            wait(OWNERS - 1)

        @pl.when(jnp.logical_not(is_owner))
        def _():
            wait(OWNERS)

    def scan(which, delay, result):
        count = (NTM - 1) * TILE
        remote(fwd_recv.at[which, pl.ds(0, count)], fwd_recv.at[which, pl.ds(0, count)],
               fs_sem.at[which], fr_sem.at[which], p, up).wait_recv()
        flat2[...] = fwd_recv[which].astype(F32)
        size = NTM * ROWS
        total = jnp.concatenate([flat2[pl.ds(g, size, stride=GROUPS), :] for g in range(GROUPS)], axis=1)
        row = lax.broadcasted_iota(jnp.int32, (size, NY), 0)

        def later(x, blocks):
            return jnp.where(row >= blocks * ROWS, pltpu.roll(x, blocks * ROWS, 0), 0.0)

        total = later(total, delay)
        for k in range(5):
            total = total + dot(later(total, 1 << k).astype(BF16), pw[k])
        for g in range(GROUPS):
            flat2[pl.ds(g, size, stride=GROUPS), :] = total[:, g * LANES:(g + 1) * LANES]
        result[...] = flat2[...].astype(result.dtype)

    def back(which, src, dst, edge, top, bottom):
        def copy(block, place, space):
            return remote(src.at[pl.ds(pl.multiple_of(block * TILE, TILE), TILE)],
                          dst.at[pl.ds(pl.multiple_of(place * TILE, TILE), TILE)],
                          bks_sem.at[which], bkr_sem.at[which], block, space)

        @pl.when(top)
        def _():
            @pl.loop(0, NTM)
            def _(i):
                copy(i, edge + OWNERS + chunk, up).start()

        @pl.when(bottom)
        def _():
            @pl.loop(0, NTM)
            def _(i):
                copy(i, chunk - (OWNERS - edge), down).start()

        @pl.loop(1, NTM)
        def _(i):
            copy(lax.rem(p + i, NTM), edge + chunk, s).start()

        at = pl.ds(pl.multiple_of((edge + chunk) * TILE, TILE), TILE)
        dst[at, :] = src[pl.ds(pl.multiple_of(p * TILE, TILE), TILE), :]

    def back_wait(which, dst, edge):
        def wait(n):
            part = dst.at[pl.ds(0, n * TILE)]
            remote(part, part, bks_sem.at[which], bkr_sem.at[which], p, up).wait_recv()

        @pl.when(is_owner)
        def _():
            wait(OWNERS + 2 * edge - 1)

        @pl.when(jnp.logical_not(is_owner))
        def _():
            wait(OWNERS + 2 * edge)

    def back_end(which, src, on_edge):
        def wait(n):
            part = src.at[pl.ds(0, n * TILE)]
            remote(part, part, bks_sem.at[which], bkr_sem.at[which], p, up).wait_send()

        @pl.when(is_owner)
        def _():
            wait(NTM - 1)

        @pl.when(on_edge)
        def _():
            wait(NTM)

    forward(0, dsend[...])
    start_shift(d_copies)

    for copy in halos[:2]:
        copy.wait_recv()
    for side, at in ((0, 0), (1, INNER + SLAB)):
        packed = fhalo[side].astype(F32)
        for k in range(STEPS):
            if k < 4:
                rows = packed[8 * k:8 * k + 8]
            elif k < 7:
                rows = packed[8 * (6 - k):8 * (7 - k)]
                rows = pltpu.roll(rows, INNER - (7 - k) if side == 0 else 7 - k, 0)
            else:
                rows = jnp.zeros((INNER, NY), F32)
            fext[k, at:at + INNER, :] = rows

    begin = jnp.where(first, uin[8:72, :], jnp.zeros((64, NY), F32))
    bsend[...] = sweep(begin, weights64, True)[8:56]

    @pl.when(is_owner)
    def _():
        scan(0, 2, back1_send)
        back(0, back1_send, back1_recv, 4, top_owner, bottom_owner)

    back_wait(0, back1_recv, 4)
    flat3[...] = back1_recv[...].astype(F32)
    before = jnp.concatenate([flat3[pl.ds(g, 80, stride=GROUPS), :] for g in range(GROUPS)], axis=1)

    carry[...] = dot3(before[8:72], pw[0], cl[...])
    v = advance(before, weights80(), None)
    previous_w = lax.fori_loop(1, STEPS, lambda k, v: advance(v, weights80(), None), v)[8:72]
    end_shift(d_copies, drecv)
    carried = carry[...]
    pair = jnp.concatenate([previous_w - carried, drecv[...] + carried], axis=0)
    drecv[...] = brecv[...] + drecv[...] + previous_w
    pair = sweep(pair, weights128, False)
    residual = pair[8:56]
    forward(1, residual)
    out[7] = bsend[...] + dsend[...] + pair[72:120] + residual

    @pl.when(is_owner)
    def _():
        scan(1, 1, back2_send)
        back(1, back2_send, back2_recv, 2, top2_owner, bottom2_owner)

    back_wait(1, back2_recv, 2)
    correction = jnp.concatenate([back2_recv[pl.ds(g, 64, stride=GROUPS), :] for g in range(GROUPS)], axis=1)
    v = jnp.where(first, uin[8:72, :], drecv[...] + correction)
    end = out[7] + dot3(correction[8:56], pw[0], cl[...])
    v = advance(v, weights64(), fext[0])
    out[7] = end
    out[0] = v[8:56]

    def last(k, v):
        v = advance(v, weights64(), fext[k])
        out[k] = v[8:56]
        return v

    lax.fori_loop(1, STEPS - 1, last, v)

    for sent in halos:
        sent.wait_send()

    @pl.when(starts)
    def _():
        for sent in u_halos:
            sent.wait_send()

    @pl.when(p < NTM - 1)
    def _():
        for sent in ahead + d_copies:
            sent.wait_send()

    forward_end(0)
    forward_end(1)
    back_end(0, back1_send, top_owner | bottom_owner)
    back_end(1, back2_send, top2_owner | bottom2_owner)


def per_device(initial_state, velocity, diffusion, forcing, implicit, coarse_implicit):
    V = pltpu.VMEM
    DMA = pltpu.SemaphoreType.DMA
    square = (NY, NY)
    scratch = [
        V(square, F32), V(square, F32), V(square, BF16), V(square, BF16), V(square, BF16),
        V((5,) + square, BF16), V(square, BF16), V(square, F32),
        V((STEPS, SLAB, NY), BF16), V((80, NY), BF16), V((80, NY), BF16), V((80, NY), F32),
        V((2, 32, NY), BF16), V((2, 32, NY), BF16),
        V((3, 80, NY), F32), V((STEPS, 64, NY), F32),
        V((STEPS, 80, NY), BF16),
        V((SLAB, NY), F32), V((64, NY), F32), V((SLAB, NY), F32), V((64, NY), F32),
        V((SLAB * GROUPS, LANES), F32), V((2, SLAB * GROUPS, LANES), BF16),
        V((2, NTM * TILE, LANES), BF16), V((NTM * TILE, LANES), F32),
        V((NTM * TILE, LANES), BF16), V((80 * GROUPS, LANES), BF16), V((80 * GROUPS, LANES), F32),
        V((NTM * TILE, LANES), F32), V((64 * GROUPS, LANES), F32), V((80, NY), F32), V((64, NY), F32),
        DMA((6,)), DMA((6,)), DMA((6,)), DMA((2,)), DMA((2,)), DMA((9,)), DMA((9,)),
        DMA((2,)), DMA((2,)), DMA((2,)), DMA((2,)),
    ]
    return pl.pallas_call(
        kernel,
        out_shape=jax.ShapeDtypeStruct((STEPS, SLAB, NY), F32),
        in_specs=[pl.BlockSpec(memory_space=pl.ANY)] * 6,
        out_specs=pl.BlockSpec(memory_space=pltpu.VMEM),
        scratch_shapes=scratch,
        compiler_params=pltpu.CompilerParams(
            collective_id=0, has_side_effects=True, vmem_limit_bytes=40 * 2**20),
    )(*[pltpu.with_memory_space_constraint(x, pltpu.HBM)
        for x in (initial_state, velocity, diffusion, forcing, implicit, coarse_implicit)])


def solution(mesh):
    in_specs = (
        P("space", None),
        P("space", None),
        P("space", None),
        P("tm", "space", None),
        P(),
        P(),
    )
    return jax.shard_map(
        per_device, mesh=mesh, in_specs=in_specs, out_specs=P("tm", "space", None), check_vma=False
    )
```

```python
import functools

import jax
import jax.numpy as jnp
from jax import lax
from jax.experimental import pallas as pl
from jax.experimental.pallas import tpu as pltpu
from jax.sharding import PartitionSpec as P

F32, BF16 = jnp.float32, jnp.bfloat16
MESH = pl.DeviceIdType.MESH

STEPS = 8
NTM = 32
SLAB = 48
NY = 512
LANES = 128
GROUPS = NY // LANES
OWNERS = 12
ROWS = SLAB // OWNERS
TILE = ROWS * GROUPS
OUTER = 16
INNER = 8


OWNER_OF = (8, 10, 12, 14, 9, 13, 19, 23, 16, 18, 20, 22)


def owner_of(chunk):
    return OWNER_OF[chunk]


def split(x):
    high = x.astype(BF16)
    return high, (x - high.astype(F32)).astype(BF16)


def dot(a, b):
    return jnp.dot(a, b, preferred_element_type=F32)


def dot3(x, high, low):
    rows = x.shape[0]
    xh, xl = split(x)
    both = dot(jnp.concatenate([xh, xl], axis=0), high)
    return both[:rows] + both[rows:] + dot(xh, low)


def kernel(u0_hbm, vel_hbm, dif_hbm, forcing_hbm, imp_hbm, coarse_hbm, out,
           mv, cv, mh, ml, cl, pw, plow, ptmp, fin, vin, din, uin, fpack, fhalo,
           wext, fext, bsend, brecv, dsend, drecv, flat, fwd_send, fwd_recv, flat2,
           back1_send, back1_recv, flat3, back2_send, back2_recv, chold,
           in_sem, halo_send, halo_recv, u_send, u_recv, sh_send, sh_recv,
           fs_sem, fr_sem, bks_sem, bkr_sem):
    p = lax.axis_index("tm")
    s = lax.axis_index("space")
    nsp = lax.axis_size("space")
    up = lax.rem(s + nsp - 1, nsp)
    down = lax.rem(s + 1, nsp)
    first = p == 0
    chunk = jnp.int32(-1)
    for j in range(OWNERS):
        chunk = jnp.where(p == OWNER_OF[j], j, chunk)
    is_owner = chunk >= 0
    top_owner = is_owner & (chunk < 4)
    bottom_owner = is_owner & (chunk >= OWNERS - 4)
    top2_owner = is_owner & (chunk < 2)
    bottom2_owner = is_owner & (chunk >= OWNERS - 2)

    loads = [
        pltpu.make_async_copy(forcing_hbm, fin, in_sem.at[0]),
        pltpu.make_async_copy(imp_hbm, mv, in_sem.at[1]),
        pltpu.make_async_copy(vel_hbm, vin.at[pl.ds(OUTER, SLAB)], in_sem.at[2]),
        pltpu.make_async_copy(dif_hbm, din.at[pl.ds(OUTER, SLAB)], in_sem.at[3]),
        pltpu.make_async_copy(u0_hbm, uin.at[pl.ds(INNER, SLAB)], in_sem.at[4]),
        pltpu.make_async_copy(coarse_hbm, cv, in_sem.at[5]),
    ]
    for load in loads:
        load.start()

    barrier = pltpu.get_barrier_semaphore()

    def greet(tm, space):
        pl.semaphore_signal(barrier, inc=1, device_id=(tm, space), device_id_type=MESH)

    greet(p, up)
    greet(p, down)

    @pl.when(p > 0)
    def _():
        for other in (up, s, down):
            greet(p - 1, other)

    @pl.when(is_owner)
    def _():
        @pl.loop(1, NTM)
        def _(i):
            greet(lax.rem(p + i, NTM), s)

    total = 2 + OWNERS - jnp.where(is_owner, 1, 0) + jnp.where(p < NTM - 1, 3, 0)
    pl.semaphore_wait(barrier, total)

    def remote(src, dst, send, recv, tm, space):
        return pltpu.make_async_remote_copy(src_ref=src, dst_ref=dst, send_sem=send, recv_sem=recv,
                                            device_id=(tm, space), device_id_type=MESH)

    edge_low, edge_high = pl.ds(0, OUTER), pl.ds(OUTER + SLAB, OUTER)
    own_low, own_high = pl.ds(0, 16), pl.ds(SLAB - 16, 16)
    halos = [
        remote(fpack.at[0], fhalo.at[0], halo_send.at[0], halo_recv.at[0], p, down),
        remote(fpack.at[1], fhalo.at[1], halo_send.at[1], halo_recv.at[1], p, up),
        remote(vel_hbm.at[own_high], vin.at[edge_low], halo_send.at[2], halo_recv.at[2], p, down),
        remote(vel_hbm.at[own_low], vin.at[edge_high], halo_send.at[3], halo_recv.at[3], p, up),
        remote(dif_hbm.at[own_high], din.at[edge_low], halo_send.at[4], halo_recv.at[4], p, down),
        remote(dif_hbm.at[own_low], din.at[edge_high], halo_send.at[5], halo_recv.at[5], p, up),
    ]
    for copy in halos[2:]:
        copy.start()
    u_halos = [
        remote(u0_hbm.at[pl.ds(SLAB - INNER, INNER)], uin.at[pl.ds(0, INNER)], u_send.at[0], u_recv.at[0], p, down),
        remote(u0_hbm.at[pl.ds(0, INNER)], uin.at[pl.ds(INNER + SLAB, INNER)], u_send.at[1], u_recv.at[1], p, up),
    ]

    @pl.when(first)
    def _():
        for copy in u_halos:
            copy.start()

    loads[0].wait()
    sub = lax.broadcasted_iota(jnp.int32, (INNER, NY), 0)
    lower = [fin[k, SLAB - 16:SLAB, :].astype(F32)[8:] for k in range(7)]
    upper = [fin[k, 0:16, :].astype(F32)[:8] for k in range(7)]
    for side, rows in ((0, lower), (1, upper)):
        packed = []
        for k in range(4):
            if k == 3:
                packed.append(rows[3])
                continue
            count = k + 1
            if side == 0:
                moved = pltpu.roll(rows[6 - k], count, 0)
                packed.append(jnp.where(sub < count, moved, rows[k]))
            else:
                moved = pltpu.roll(rows[6 - k], INNER - count, 0)
                packed.append(jnp.where(sub >= INNER - count, moved, rows[k]))
        fpack[side] = jnp.concatenate(packed, axis=0).astype(BF16)

    for copy in halos[:2]:
        copy.start()

    loads[1].wait()
    a, b = split(mv[...])
    mh[...] = a
    ml[...] = b
    loads[5].wait()
    a, b = split(cv[...])
    pw[0] = a
    cl[...] = b
    plow[...] = b
    for k in range(STEPS):
        fext[k, INNER:INNER + SLAB, :] = fin[k].astype(F32)

    def square(k):
        @pl.loop(0, 4)
        def _(i):
            rows = pl.ds(pl.multiple_of(i * 128, 128), 128)
            xh, xl = pw[k - 1, rows, :], plow[rows, :]
            both = dot(jnp.concatenate([xh, xl], axis=0), pw[k - 1])
            ptmp[rows, :] = both[:128] + both[128:] + dot(xh, plow[...])

        high, low = split(ptmp[...])
        pw[k] = high
        plow[...] = low

    @pl.when(is_owner)
    def _():
        square(1)
        square(2)

    for load in loads[2:5]:
        load.wait()
    for copy in halos:
        copy.wait_recv()

    spread = din[...].astype(F32)
    half = 0.5 * vin[...].astype(F32)
    wext[0] = spread + half
    wext[1] = 1.0 - 2.0 * spread
    wext[2] = spread - half
    for side, at in ((0, 0), (1, INNER + SLAB)):
        packed = fhalo[side].astype(F32)
        for k in range(STEPS):
            if k < 4:
                rows = packed[8 * k:8 * k + 8]
            elif k < 7:
                rows = packed[8 * (6 - k):8 * (7 - k)]
                rows = pltpu.roll(rows, INNER - (7 - k) if side == 0 else 7 - k, 0)
            else:
                rows = jnp.zeros((INNER, NY), F32)
            fext[k, at:at + INNER, :] = rows

    @pl.when(first)
    def _():
        for copy in u_halos:
            copy.wait_recv()

    def advance(v, weights, forced):
        west, centre, east = weights
        rows = v.shape[0]
        mixed = centre * v + east * pltpu.roll(v, rows - 1, 0) + west * pltpu.roll(v, 1, 0)
        if forced is not None:
            mixed = mixed + forced
        return dot3(mixed, mh[...], ml[...])

    def weights64():
        return tuple(wext[i, 8:72, :] for i in range(3))

    def sweep(v, weights, forced):
        def turn(k, v):
            return advance(v, weights(), fext[k] if forced else None)
        return lax.fori_loop(0, STEPS, turn, v)

    def weights128():
        return tuple(jnp.concatenate([w, w], axis=0) for w in weights64())

    def weights80():
        return tuple(wext[i] for i in range(3))

    def shift(src, dst, at):
        return [
            remote(src, dst.at[pl.ds(INNER, SLAB)], sh_send.at[at], sh_recv.at[at], p + 1, s),
            remote(src.at[pl.ds(0, INNER)], dst.at[pl.ds(INNER + SLAB, INNER)],
                   sh_send.at[at + 1], sh_recv.at[at + 1], p + 1, up),
            remote(src.at[pl.ds(SLAB - INNER, INNER)], dst.at[pl.ds(0, INNER)],
                   sh_send.at[at + 2], sh_recv.at[at + 2], p + 1, down),
        ]

    def start_shift(copies):
        @pl.when(p < NTM - 1)
        def _():
            for copy in copies:
                copy.start()

    def end_shift(copies, dst):
        @pl.when(p > 0)
        def _():
            for copy in copies:
                copy.wait_recv()

        @pl.when(first)
        def _():
            dst[...] = jnp.zeros_like(dst)

    begin = jnp.where(first, uin[...], jnp.zeros((64, NY), F32))
    bsend[...] = sweep(begin, weights64, True)[8:56]
    b_copies = shift(bsend, brecv, 0)
    start_shift(b_copies)

    @pl.when(is_owner)
    def _():
        square(3)
        square(4)

    end_shift(b_copies, brecv)
    dsend[...] = sweep(brecv[...], weights64, False)[8:56]
    d_copies = shift(dsend, drecv, 3)

    def forward(which, rows):
        for g in range(GROUPS):
            flat[pl.ds(g, SLAB, stride=GROUPS), :] = rows[:, g * LANES:(g + 1) * LANES]
        fwd_send[which] = flat[...].astype(BF16)
        mine = pl.ds(pl.multiple_of(p * TILE, TILE), TILE)
        for j in range(OWNERS):
            part = pl.ds(j * TILE, TILE)
            copy = remote(fwd_send.at[which, part], fwd_recv.at[which, mine],
                          fs_sem.at[which], fr_sem.at[which], owner_of(j), s)

            @pl.when(p != owner_of(j))
            def _():
                copy.start()

            @pl.when(p == owner_of(j))
            def _():
                fwd_recv[which, mine, :] = fwd_send[which, part, :]

    def forward_end(which):
        def wait(n):
            remote(fwd_send.at[which, pl.ds(0, n * TILE)], fwd_recv.at[which, pl.ds(0, n * TILE)],
                   fs_sem.at[which], fr_sem.at[which], p, up).wait_send()

        @pl.when(is_owner)
        def _():
            wait(OWNERS - 1)

        @pl.when(jnp.logical_not(is_owner))
        def _():
            wait(OWNERS)

    def scan(which, delay, result):
        count = (NTM - 1) * TILE
        remote(fwd_recv.at[which, pl.ds(0, count)], fwd_recv.at[which, pl.ds(0, count)],
               fs_sem.at[which], fr_sem.at[which], p, up).wait_recv()
        flat2[...] = fwd_recv[which].astype(F32)
        size = NTM * ROWS
        total = jnp.concatenate([flat2[pl.ds(g, size, stride=GROUPS), :] for g in range(GROUPS)], axis=1)
        row = lax.broadcasted_iota(jnp.int32, (size, NY), 0)

        def later(x, blocks):
            return jnp.where(row >= blocks * ROWS, pltpu.roll(x, blocks * ROWS, 0), 0.0)

        total = later(total, delay)
        for k in range(5):
            total = total + dot(later(total, 1 << k).astype(BF16), pw[k])
        for g in range(GROUPS):
            flat2[pl.ds(g, size, stride=GROUPS), :] = total[:, g * LANES:(g + 1) * LANES]
        result[...] = flat2[...].astype(result.dtype)

    def back(which, src, dst, edge, top, bottom):
        def copy(block, place, space):
            return remote(src.at[pl.ds(pl.multiple_of(block * TILE, TILE), TILE)],
                          dst.at[pl.ds(pl.multiple_of(place * TILE, TILE), TILE)],
                          bks_sem.at[which], bkr_sem.at[which], block, space)

        @pl.when(top)
        def _():
            @pl.loop(0, NTM)
            def _(i):
                copy(i, edge + OWNERS + chunk, up).start()

        @pl.when(bottom)
        def _():
            @pl.loop(0, NTM)
            def _(i):
                copy(i, chunk - (OWNERS - edge), down).start()

        @pl.loop(1, NTM)
        def _(i):
            copy(lax.rem(p + i, NTM), edge + chunk, s).start()

        at = pl.ds(pl.multiple_of((edge + chunk) * TILE, TILE), TILE)
        dst[at, :] = src[pl.ds(pl.multiple_of(p * TILE, TILE), TILE), :]

    def back_wait(which, dst, edge):
        def wait(n):
            part = dst.at[pl.ds(0, n * TILE)]
            remote(part, part, bks_sem.at[which], bkr_sem.at[which], p, up).wait_recv()

        @pl.when(is_owner)
        def _():
            wait(OWNERS + 2 * edge - 1)

        @pl.when(jnp.logical_not(is_owner))
        def _():
            wait(OWNERS + 2 * edge)

    def back_end(which, src, on_edge):
        def wait(n):
            part = src.at[pl.ds(0, n * TILE)]
            remote(part, part, bks_sem.at[which], bkr_sem.at[which], p, up).wait_send()

        @pl.when(is_owner)
        def _():
            wait(NTM - 1)

        @pl.when(on_edge)
        def _():
            wait(NTM)

    forward(0, dsend[...])
    start_shift(d_copies)

    @pl.when(is_owner)
    def _():
        scan(0, 2, back1_send)
        back(0, back1_send, back1_recv, 4, top_owner, bottom_owner)

    back_wait(0, back1_recv, 4)
    flat3[...] = back1_recv[...].astype(F32)
    before = jnp.concatenate([flat3[pl.ds(g, 80, stride=GROUPS), :] for g in range(GROUPS)], axis=1)

    chold[...] = dot3(before[8:72], pw[0], cl[...])
    v = advance(before, weights80(), None)
    previous_w = lax.fori_loop(1, STEPS, lambda k, v: advance(v, weights80(), None), v)[8:72]
    end_shift(d_copies, drecv)
    carried = chold[...]
    pair = jnp.concatenate([previous_w - carried, drecv[...] + carried], axis=0)
    drecv[...] = brecv[...] + drecv[...] + previous_w
    pair = sweep(pair, weights128, False)
    residual = pair[8:56]
    forward(1, residual)
    out[7] = bsend[...] + dsend[...] + pair[72:120] + residual

    @pl.when(is_owner)
    def _():
        scan(1, 1, back2_send)
        back(1, back2_send, back2_recv, 2, top2_owner, bottom2_owner)

    back_wait(1, back2_recv, 2)
    correction = jnp.concatenate([back2_recv[pl.ds(g, 64, stride=GROUPS), :] for g in range(GROUPS)], axis=1)
    v = jnp.where(first, uin[...], drecv[...] + correction)
    end = out[7] + dot3(correction[8:56], pw[0], cl[...])
    v = advance(v, weights64(), fext[0])
    out[7] = end
    out[0] = v[8:56]

    def last(k, v):
        v = advance(v, weights64(), fext[k])
        out[k] = v[8:56]
        return v

    lax.fori_loop(1, STEPS - 1, last, v)

    for sent in halos:
        sent.wait_send()

    @pl.when(first)
    def _():
        for sent in u_halos:
            sent.wait_send()

    @pl.when(p < NTM - 1)
    def _():
        for sent in b_copies + d_copies:
            sent.wait_send()

    forward_end(0)
    forward_end(1)
    back_end(0, back1_send, top_owner | bottom_owner)
    back_end(1, back2_send, top2_owner | bottom2_owner)


def per_device(initial_state, velocity, diffusion, forcing, implicit, coarse_implicit):
    V = pltpu.VMEM
    DMA = pltpu.SemaphoreType.DMA
    square = (NY, NY)
    scratch = [
        V(square, F32), V(square, F32), V(square, BF16), V(square, BF16), V(square, BF16),
        V((5,) + square, BF16), V(square, BF16), V(square, F32),
        V((STEPS, SLAB, NY), BF16), V((80, NY), BF16), V((80, NY), BF16), V((64, NY), F32),
        V((2, 32, NY), BF16), V((2, 32, NY), BF16),
        V((3, 80, NY), F32), V((STEPS, 64, NY), F32),
        V((SLAB, NY), F32), V((64, NY), F32), V((SLAB, NY), F32), V((64, NY), F32),
        V((SLAB * GROUPS, LANES), F32), V((2, SLAB * GROUPS, LANES), BF16),
        V((2, NTM * TILE, LANES), BF16), V((NTM * TILE, LANES), F32),
        V((NTM * TILE, LANES), BF16), V((80 * GROUPS, LANES), BF16), V((80 * GROUPS, LANES), F32),
        V((NTM * TILE, LANES), F32), V((64 * GROUPS, LANES), F32), V((64, NY), F32),
        DMA((6,)), DMA((6,)), DMA((6,)), DMA((2,)), DMA((2,)), DMA((6,)), DMA((6,)),
        DMA((2,)), DMA((2,)), DMA((2,)), DMA((2,)),
    ]
    return pl.pallas_call(
        kernel,
        out_shape=jax.ShapeDtypeStruct((STEPS, SLAB, NY), F32),
        in_specs=[pl.BlockSpec(memory_space=pl.ANY)] * 6,
        out_specs=pl.BlockSpec(memory_space=pltpu.VMEM),
        scratch_shapes=scratch,
        compiler_params=pltpu.CompilerParams(
            collective_id=0, has_side_effects=True, vmem_limit_bytes=40 * 2**20),
    )(*[pltpu.with_memory_space_constraint(x, pltpu.HBM)
        for x in (initial_state, velocity, diffusion, forcing, implicit, coarse_implicit)])


def solution(mesh):
    in_specs = (
        P("space", None),
        P("space", None),
        P("space", None),
        P("tm", "space", None),
        P(),
        P(),
    )
    return jax.shard_map(
        per_device, mesh=mesh, in_specs=in_specs, out_specs=P("tm", "space", None), check_vma=False
    )
```

```python
import functools

import jax
import jax.numpy as jnp
from jax import lax
from jax.experimental import pallas as pl
from jax.experimental.pallas import tpu as pltpu
from jax.sharding import PartitionSpec as P

F32, BF16 = jnp.float32, jnp.bfloat16
MESH = pl.DeviceIdType.MESH

STEPS = 8
NTM = 32
SLAB = 48
NY = 512
LANES = 128
GROUPS = NY // LANES
OWNERS = 12
ROWS = SLAB // OWNERS
TILE = ROWS * GROUPS
OUTER = 16
INNER = 8


OWNER_OF = (8, 10, 12, 14, 9, 13, 19, 23, 16, 18, 20, 22)


def owner_of(chunk):
    return OWNER_OF[chunk]


def split(x):
    high = x.astype(BF16)
    return high, (x - high.astype(F32)).astype(BF16)


def dot(a, b):
    return jnp.dot(a, b, preferred_element_type=F32)


def dot3(x, high, low):
    rows = x.shape[0]
    xh, xl = split(x)
    both = dot(jnp.concatenate([xh, xl], axis=0), high)
    return both[:rows] + both[rows:] + dot(xh, low)


def kernel(u0_hbm, vel_hbm, dif_hbm, forcing_hbm, imp_hbm, coarse_hbm, out,
           mv, cv, mh, ml, cl, pw, plow, ptmp, fin, vin, din, uin, fpack, fhalo,
           wext, fext, bsend, brecv, dsend, drecv, flat, fwd_send, fwd_recv, flat2,
           back1_send, back1_recv, flat3, back2_send, back2_recv, chold, whold,
           in_sem, halo_send, halo_recv, u_send, u_recv, sh_send, sh_recv,
           fs_sem, fr_sem, bks_sem, bkr_sem):
    p = lax.axis_index("tm")
    s = lax.axis_index("space")
    nsp = lax.axis_size("space")
    up = lax.rem(s + nsp - 1, nsp)
    down = lax.rem(s + 1, nsp)
    first = p == 0
    chunk = jnp.int32(-1)
    for j in range(OWNERS):
        chunk = jnp.where(p == OWNER_OF[j], j, chunk)
    is_owner = chunk >= 0
    top_owner = is_owner & (chunk < 4)
    bottom_owner = is_owner & (chunk >= OWNERS - 4)
    top2_owner = is_owner & (chunk < 2)
    bottom2_owner = is_owner & (chunk >= OWNERS - 2)

    loads = [
        pltpu.make_async_copy(forcing_hbm, fin, in_sem.at[0]),
        pltpu.make_async_copy(imp_hbm, mv, in_sem.at[1]),
        pltpu.make_async_copy(vel_hbm, vin.at[pl.ds(OUTER, SLAB)], in_sem.at[2]),
        pltpu.make_async_copy(dif_hbm, din.at[pl.ds(OUTER, SLAB)], in_sem.at[3]),
        pltpu.make_async_copy(u0_hbm, uin.at[pl.ds(INNER, SLAB)], in_sem.at[4]),
        pltpu.make_async_copy(coarse_hbm, cv, in_sem.at[5]),
    ]
    for load in loads:
        load.start()

    barrier = pltpu.get_barrier_semaphore()

    def greet(tm, space):
        pl.semaphore_signal(barrier, inc=1, device_id=(tm, space), device_id_type=MESH)

    greet(p, up)
    greet(p, down)

    @pl.when(p > 0)
    def _():
        for other in (up, s, down):
            greet(p - 1, other)

    @pl.when(is_owner)
    def _():
        @pl.loop(1, NTM)
        def _(i):
            greet(lax.rem(p + i, NTM), s)

    total = 2 + OWNERS - jnp.where(is_owner, 1, 0) + jnp.where(p < NTM - 1, 3, 0)
    pl.semaphore_wait(barrier, total)

    def remote(src, dst, send, recv, tm, space):
        return pltpu.make_async_remote_copy(src_ref=src, dst_ref=dst, send_sem=send, recv_sem=recv,
                                            device_id=(tm, space), device_id_type=MESH)

    edge_low, edge_high = pl.ds(0, OUTER), pl.ds(OUTER + SLAB, OUTER)
    own_low, own_high = pl.ds(0, 16), pl.ds(SLAB - 16, 16)
    halos = [
        remote(fpack.at[0], fhalo.at[0], halo_send.at[0], halo_recv.at[0], p, down),
        remote(fpack.at[1], fhalo.at[1], halo_send.at[1], halo_recv.at[1], p, up),
        remote(vel_hbm.at[own_high], vin.at[edge_low], halo_send.at[2], halo_recv.at[2], p, down),
        remote(vel_hbm.at[own_low], vin.at[edge_high], halo_send.at[3], halo_recv.at[3], p, up),
        remote(dif_hbm.at[own_high], din.at[edge_low], halo_send.at[4], halo_recv.at[4], p, down),
        remote(dif_hbm.at[own_low], din.at[edge_high], halo_send.at[5], halo_recv.at[5], p, up),
    ]
    for copy in halos[2:]:
        copy.start()
    u_halos = [
        remote(u0_hbm.at[pl.ds(SLAB - INNER, INNER)], uin.at[pl.ds(0, INNER)], u_send.at[0], u_recv.at[0], p, down),
        remote(u0_hbm.at[pl.ds(0, INNER)], uin.at[pl.ds(INNER + SLAB, INNER)], u_send.at[1], u_recv.at[1], p, up),
    ]

    @pl.when(first)
    def _():
        for copy in u_halos:
            copy.start()

    loads[0].wait()
    sub = lax.broadcasted_iota(jnp.int32, (INNER, NY), 0)
    lower = [fin[k, SLAB - 16:SLAB, :].astype(F32)[8:] for k in range(7)]
    upper = [fin[k, 0:16, :].astype(F32)[:8] for k in range(7)]
    for side, rows in ((0, lower), (1, upper)):
        packed = []
        for k in range(4):
            if k == 3:
                packed.append(rows[3])
                continue
            count = k + 1
            if side == 0:
                moved = pltpu.roll(rows[6 - k], count, 0)
                packed.append(jnp.where(sub < count, moved, rows[k]))
            else:
                moved = pltpu.roll(rows[6 - k], INNER - count, 0)
                packed.append(jnp.where(sub >= INNER - count, moved, rows[k]))
        fpack[side] = jnp.concatenate(packed, axis=0).astype(BF16)

    for copy in halos[:2]:
        copy.start()

    loads[1].wait()
    a, b = split(mv[...])
    mh[...] = a
    ml[...] = b
    loads[5].wait()
    a, b = split(cv[...])
    pw[0] = a
    cl[...] = b
    plow[...] = b
    for k in range(STEPS):
        fext[k, INNER:INNER + SLAB, :] = fin[k].astype(F32)

    def square(k):
        @pl.loop(0, 4)
        def _(i):
            rows = pl.ds(pl.multiple_of(i * 128, 128), 128)
            xh, xl = pw[k - 1, rows, :], plow[rows, :]
            both = dot(jnp.concatenate([xh, xl], axis=0), pw[k - 1])
            ptmp[rows, :] = both[:128] + both[128:] + dot(xh, plow[...])

        high, low = split(ptmp[...])
        pw[k] = high
        plow[...] = low

    @pl.when(is_owner)
    def _():
        square(1)
        square(2)

    for load in loads[2:5]:
        load.wait()
    for copy in halos:
        copy.wait_recv()

    spread = din[...].astype(F32)
    half = 0.5 * vin[...].astype(F32)
    wext[0] = spread + half
    wext[1] = 1.0 - 2.0 * spread
    wext[2] = spread - half
    for side, at in ((0, 0), (1, INNER + SLAB)):
        packed = fhalo[side].astype(F32)
        for k in range(STEPS):
            if k < 4:
                rows = packed[8 * k:8 * k + 8]
            elif k < 7:
                rows = packed[8 * (6 - k):8 * (7 - k)]
                rows = pltpu.roll(rows, INNER - (7 - k) if side == 0 else 7 - k, 0)
            else:
                rows = jnp.zeros((INNER, NY), F32)
            fext[k, at:at + INNER, :] = rows

    @pl.when(first)
    def _():
        for copy in u_halos:
            copy.wait_recv()

    def advance(v, weights, forced):
        west, centre, east = weights
        rows = v.shape[0]
        mixed = centre * v + east * pltpu.roll(v, rows - 1, 0) + west * pltpu.roll(v, 1, 0)
        if forced is not None:
            mixed = mixed + forced
        return dot3(mixed, mh[...], ml[...])

    def weights64():
        return tuple(wext[i, 8:72, :] for i in range(3))

    def sweep(v, weights, forced):
        def turn(k, v):
            return advance(v, weights(), fext[k] if forced else None)
        return lax.fori_loop(0, STEPS, turn, v)

    def weights80():
        return tuple(wext[i] for i in range(3))

    def shift(src, dst, at):
        return [
            remote(src, dst.at[pl.ds(INNER, SLAB)], sh_send.at[at], sh_recv.at[at], p + 1, s),
            remote(src.at[pl.ds(0, INNER)], dst.at[pl.ds(INNER + SLAB, INNER)],
                   sh_send.at[at + 1], sh_recv.at[at + 1], p + 1, up),
            remote(src.at[pl.ds(SLAB - INNER, INNER)], dst.at[pl.ds(0, INNER)],
                   sh_send.at[at + 2], sh_recv.at[at + 2], p + 1, down),
        ]

    def start_shift(copies):
        @pl.when(p < NTM - 1)
        def _():
            for copy in copies:
                copy.start()

    def end_shift(copies, dst):
        @pl.when(p > 0)
        def _():
            for copy in copies:
                copy.wait_recv()

        @pl.when(first)
        def _():
            dst[...] = jnp.zeros_like(dst)

    begin = jnp.where(first, uin[...], jnp.zeros((64, NY), F32))
    bsend[...] = sweep(begin, weights64, True)[8:56]
    b_copies = shift(bsend, brecv, 0)
    start_shift(b_copies)

    @pl.when(is_owner)
    def _():
        square(3)
        square(4)

    end_shift(b_copies, brecv)
    dsend[...] = sweep(brecv[...], weights64, False)[8:56]
    d_copies = shift(dsend, drecv, 3)

    def forward(which, rows):
        for g in range(GROUPS):
            flat[pl.ds(g, SLAB, stride=GROUPS), :] = rows[:, g * LANES:(g + 1) * LANES]
        fwd_send[which] = flat[...].astype(BF16)
        mine = pl.ds(pl.multiple_of(p * TILE, TILE), TILE)
        for j in range(OWNERS):
            part = pl.ds(j * TILE, TILE)
            copy = remote(fwd_send.at[which, part], fwd_recv.at[which, mine],
                          fs_sem.at[which], fr_sem.at[which], owner_of(j), s)

            @pl.when(p != owner_of(j))
            def _():
                copy.start()

            @pl.when(p == owner_of(j))
            def _():
                fwd_recv[which, mine, :] = fwd_send[which, part, :]

    def forward_end(which):
        def wait(n):
            remote(fwd_send.at[which, pl.ds(0, n * TILE)], fwd_recv.at[which, pl.ds(0, n * TILE)],
                   fs_sem.at[which], fr_sem.at[which], p, up).wait_send()

        @pl.when(is_owner)
        def _():
            wait(OWNERS - 1)

        @pl.when(jnp.logical_not(is_owner))
        def _():
            wait(OWNERS)

    def scan(which, delay, result):
        count = (NTM - 1) * TILE
        remote(fwd_recv.at[which, pl.ds(0, count)], fwd_recv.at[which, pl.ds(0, count)],
               fs_sem.at[which], fr_sem.at[which], p, up).wait_recv()
        flat2[...] = fwd_recv[which].astype(F32)
        size = NTM * ROWS
        total = jnp.concatenate([flat2[pl.ds(g, size, stride=GROUPS), :] for g in range(GROUPS)], axis=1)
        row = lax.broadcasted_iota(jnp.int32, (size, NY), 0)

        def later(x, blocks):
            return jnp.where(row >= blocks * ROWS, pltpu.roll(x, blocks * ROWS, 0), 0.0)

        total = later(total, delay)
        for k in range(5):
            total = total + dot(later(total, 1 << k).astype(BF16), pw[k])
        for g in range(GROUPS):
            flat2[pl.ds(g, size, stride=GROUPS), :] = total[:, g * LANES:(g + 1) * LANES]
        result[...] = flat2[...].astype(result.dtype)

    def back(which, src, dst, edge, top, bottom):
        def copy(block, place, space):
            return remote(src.at[pl.ds(pl.multiple_of(block * TILE, TILE), TILE)],
                          dst.at[pl.ds(pl.multiple_of(place * TILE, TILE), TILE)],
                          bks_sem.at[which], bkr_sem.at[which], block, space)

        @pl.when(top)
        def _():
            @pl.loop(0, NTM)
            def _(i):
                copy(i, edge + OWNERS + chunk, up).start()

        @pl.when(bottom)
        def _():
            @pl.loop(0, NTM)
            def _(i):
                copy(i, chunk - (OWNERS - edge), down).start()

        @pl.loop(1, NTM)
        def _(i):
            copy(lax.rem(p + i, NTM), edge + chunk, s).start()

        at = pl.ds(pl.multiple_of((edge + chunk) * TILE, TILE), TILE)
        dst[at, :] = src[pl.ds(pl.multiple_of(p * TILE, TILE), TILE), :]

    def back_wait(which, dst, edge):
        def wait(n):
            part = dst.at[pl.ds(0, n * TILE)]
            remote(part, part, bks_sem.at[which], bkr_sem.at[which], p, up).wait_recv()

        @pl.when(is_owner)
        def _():
            wait(OWNERS + 2 * edge - 1)

        @pl.when(jnp.logical_not(is_owner))
        def _():
            wait(OWNERS + 2 * edge)

    def back_end(which, src, on_edge):
        def wait(n):
            part = src.at[pl.ds(0, n * TILE)]
            remote(part, part, bks_sem.at[which], bkr_sem.at[which], p, up).wait_send()

        @pl.when(is_owner)
        def _():
            wait(NTM - 1)

        @pl.when(on_edge)
        def _():
            wait(NTM)

    forward(0, dsend[...])
    start_shift(d_copies)

    @pl.when(is_owner)
    def _():
        scan(0, 2, back1_send)
        back(0, back1_send, back1_recv, 4, top_owner, bottom_owner)

    back_wait(0, back1_recv, 4)
    flat3[...] = back1_recv[...].astype(F32)
    before = jnp.concatenate([flat3[pl.ds(g, 80, stride=GROUPS), :] for g in range(GROUPS)], axis=1)

    chold[...] = dot3(before[8:72], pw[0], cl[...])
    v = advance(before, weights80(), None)
    previous_w = lax.fori_loop(1, STEPS, lambda k, v: advance(v, weights80(), None), v)[8:72]
    whold[...] = previous_w
    residual = sweep(previous_w - chold[...], weights64, False)[8:56]
    forward(1, residual)
    out[7] = bsend[...] + dsend[...] + residual
    end_shift(d_copies, drecv)
    out[7] = out[7] + sweep(drecv[...] + chold[...], weights64, False)[8:56]
    drecv[...] = brecv[...] + drecv[...] + whold[...]

    @pl.when(is_owner)
    def _():
        scan(1, 1, back2_send)
        back(1, back2_send, back2_recv, 2, top2_owner, bottom2_owner)

    back_wait(1, back2_recv, 2)
    correction = jnp.concatenate([back2_recv[pl.ds(g, 64, stride=GROUPS), :] for g in range(GROUPS)], axis=1)
    v = jnp.where(first, uin[...], drecv[...] + correction)
    end = out[7] + dot3(correction[8:56], pw[0], cl[...])
    v = advance(v, weights64(), fext[0])
    out[7] = end
    out[0] = v[8:56]

    def last(k, v):
        v = advance(v, weights64(), fext[k])
        out[k] = v[8:56]
        return v

    lax.fori_loop(1, STEPS - 1, last, v)

    for sent in halos:
        sent.wait_send()

    @pl.when(first)
    def _():
        for sent in u_halos:
            sent.wait_send()

    @pl.when(p < NTM - 1)
    def _():
        for sent in b_copies + d_copies:
            sent.wait_send()

    forward_end(0)
    forward_end(1)
    back_end(0, back1_send, top_owner | bottom_owner)
    back_end(1, back2_send, top2_owner | bottom2_owner)


def per_device(initial_state, velocity, diffusion, forcing, implicit, coarse_implicit):
    V = pltpu.VMEM
    DMA = pltpu.SemaphoreType.DMA
    square = (NY, NY)
    scratch = [
        V(square, F32), V(square, F32), V(square, BF16), V(square, BF16), V(square, BF16),
        V((5,) + square, BF16), V(square, BF16), V(square, F32),
        V((STEPS, SLAB, NY), BF16), V((80, NY), BF16), V((80, NY), BF16), V((64, NY), F32),
        V((2, 32, NY), BF16), V((2, 32, NY), BF16),
        V((3, 80, NY), F32), V((STEPS, 64, NY), F32),
        V((SLAB, NY), F32), V((64, NY), F32), V((SLAB, NY), F32), V((64, NY), F32),
        V((SLAB * GROUPS, LANES), F32), V((2, SLAB * GROUPS, LANES), BF16),
        V((2, NTM * TILE, LANES), BF16), V((NTM * TILE, LANES), F32),
        V((NTM * TILE, LANES), BF16), V((80 * GROUPS, LANES), BF16), V((80 * GROUPS, LANES), F32),
        V((NTM * TILE, LANES), F32), V((64 * GROUPS, LANES), F32), V((64, NY), F32), V((64, NY), F32),
        DMA((6,)), DMA((6,)), DMA((6,)), DMA((2,)), DMA((2,)), DMA((6,)), DMA((6,)),
        DMA((2,)), DMA((2,)), DMA((2,)), DMA((2,)),
    ]
    return pl.pallas_call(
        kernel,
        out_shape=jax.ShapeDtypeStruct((STEPS, SLAB, NY), F32),
        in_specs=[pl.BlockSpec(memory_space=pl.ANY)] * 6,
        out_specs=pl.BlockSpec(memory_space=pltpu.VMEM),
        scratch_shapes=scratch,
        compiler_params=pltpu.CompilerParams(
            collective_id=0, has_side_effects=True, vmem_limit_bytes=40 * 2**20),
    )(*[pltpu.with_memory_space_constraint(x, pltpu.HBM)
        for x in (initial_state, velocity, diffusion, forcing, implicit, coarse_implicit)])


def solution(mesh):
    in_specs = (
        P("space", None),
        P("space", None),
        P("space", None),
        P("tm", "space", None),
        P(),
        P(),
    )
    return jax.shard_map(
        per_device, mesh=mesh, in_specs=in_specs, out_specs=P("tm", "space", None), check_vma=False
    )
```

```python
import functools

import jax
import jax.numpy as jnp
from jax import lax
from jax.experimental import pallas as pl
from jax.experimental.pallas import tpu as pltpu
from jax.sharding import PartitionSpec as P

F32, BF16 = jnp.float32, jnp.bfloat16
MESH = pl.DeviceIdType.MESH

STEPS = 8
NTM = 32
SLAB = 48
NY = 512
LANES = 128
GROUPS = NY // LANES
OWNERS = 12
ROWS = SLAB // OWNERS
TILE = ROWS * GROUPS
OUTER = 16
INNER = 8


OWNER_OF = (8, 10, 12, 14, 9, 13, 19, 23, 16, 18, 20, 22)


def owner_of(chunk):
    return OWNER_OF[chunk]


def split(x):
    high = x.astype(BF16)
    return high, (x - high.astype(F32)).astype(BF16)


def dot(a, b):
    return jnp.dot(a, b, preferred_element_type=F32)


def dot3(x, high, low):
    rows = x.shape[0]
    xh, xl = split(x)
    both = dot(jnp.concatenate([xh, xl], axis=0), high)
    return both[:rows] + both[rows:] + dot(xh, low)


def kernel(u0_hbm, vel_hbm, dif_hbm, forcing_hbm, imp_hbm, coarse_hbm, out,
           mv, cv, mh, ml, cl, pw, plow, ptmp, fin, vin, din, uin, fpack, fhalo,
           wext, fext, bsend, brecv, dsend, drecv, flat, fwd_send, fwd_recv, flat2,
           back1_send, back1_recv, flat3, back2_send, back2_recv, edge_send, edge_recv, chold, whold,
           in_sem, halo_send, halo_recv, u_send, u_recv, sh_send, sh_recv,
           fs_sem, fr_sem, bks_sem, bkr_sem):
    p = lax.axis_index("tm")
    s = lax.axis_index("space")
    nsp = lax.axis_size("space")
    up = lax.rem(s + nsp - 1, nsp)
    down = lax.rem(s + 1, nsp)
    first = p == 0
    chunk = jnp.int32(-1)
    for j in range(OWNERS):
        chunk = jnp.where(p == OWNER_OF[j], j, chunk)
    is_owner = chunk >= 0
    top_owner = is_owner & (chunk < 4)
    bottom_owner = is_owner & (chunk >= OWNERS - 4)
    top2_owner = is_owner & (chunk < 2)
    bottom2_owner = is_owner & (chunk >= OWNERS - 2)

    loads = [
        pltpu.make_async_copy(forcing_hbm, fin, in_sem.at[0]),
        pltpu.make_async_copy(imp_hbm, mv, in_sem.at[1]),
        pltpu.make_async_copy(vel_hbm, vin.at[pl.ds(OUTER, SLAB)], in_sem.at[2]),
        pltpu.make_async_copy(dif_hbm, din.at[pl.ds(OUTER, SLAB)], in_sem.at[3]),
        pltpu.make_async_copy(u0_hbm, uin.at[pl.ds(INNER, SLAB)], in_sem.at[4]),
        pltpu.make_async_copy(coarse_hbm, cv, in_sem.at[5]),
    ]
    for load in loads:
        load.start()

    barrier = pltpu.get_barrier_semaphore()

    def greet(tm, space):
        pl.semaphore_signal(barrier, inc=1, device_id=(tm, space), device_id_type=MESH)

    greet(p, up)
    greet(p, down)

    @pl.when(p > 0)
    def _():
        for other in (up, s, down):
            greet(p - 1, other)

    @pl.when(is_owner)
    def _():
        @pl.loop(1, NTM)
        def _(i):
            greet(lax.rem(p + i, NTM), s)

    total = 2 + OWNERS - jnp.where(is_owner, 1, 0) + jnp.where(p < NTM - 1, 3, 0)
    pl.semaphore_wait(barrier, total)

    def remote(src, dst, send, recv, tm, space):
        return pltpu.make_async_remote_copy(src_ref=src, dst_ref=dst, send_sem=send, recv_sem=recv,
                                            device_id=(tm, space), device_id_type=MESH)

    edge_low, edge_high = pl.ds(0, OUTER), pl.ds(OUTER + SLAB, OUTER)
    own_low, own_high = pl.ds(0, 16), pl.ds(SLAB - 16, 16)
    halos = [
        remote(fpack.at[0], fhalo.at[0], halo_send.at[0], halo_recv.at[0], p, down),
        remote(fpack.at[1], fhalo.at[1], halo_send.at[1], halo_recv.at[1], p, up),
        remote(vel_hbm.at[own_high], vin.at[edge_low], halo_send.at[2], halo_recv.at[2], p, down),
        remote(vel_hbm.at[own_low], vin.at[edge_high], halo_send.at[3], halo_recv.at[3], p, up),
        remote(dif_hbm.at[own_high], din.at[edge_low], halo_send.at[4], halo_recv.at[4], p, down),
        remote(dif_hbm.at[own_low], din.at[edge_high], halo_send.at[5], halo_recv.at[5], p, up),
    ]
    for copy in halos[2:]:
        copy.start()
    u_halos = [
        remote(u0_hbm.at[pl.ds(SLAB - INNER, INNER)], uin.at[pl.ds(0, INNER)], u_send.at[0], u_recv.at[0], p, down),
        remote(u0_hbm.at[pl.ds(0, INNER)], uin.at[pl.ds(INNER + SLAB, INNER)], u_send.at[1], u_recv.at[1], p, up),
    ]

    @pl.when(first)
    def _():
        for copy in u_halos:
            copy.start()

    loads[0].wait()
    sub = lax.broadcasted_iota(jnp.int32, (INNER, NY), 0)
    lower = [fin[k, SLAB - 16:SLAB, :].astype(F32)[8:] for k in range(7)]
    upper = [fin[k, 0:16, :].astype(F32)[:8] for k in range(7)]
    for side, rows in ((0, lower), (1, upper)):
        packed = []
        for k in range(4):
            if k == 3:
                packed.append(rows[3])
                continue
            count = k + 1
            if side == 0:
                moved = pltpu.roll(rows[6 - k], count, 0)
                packed.append(jnp.where(sub < count, moved, rows[k]))
            else:
                moved = pltpu.roll(rows[6 - k], INNER - count, 0)
                packed.append(jnp.where(sub >= INNER - count, moved, rows[k]))
        fpack[side] = jnp.concatenate(packed, axis=0).astype(BF16)

    for copy in halos[:2]:
        copy.start()

    loads[1].wait()
    a, b = split(mv[...])
    mh[...] = a
    ml[...] = b
    loads[5].wait()
    a, b = split(cv[...])
    pw[0] = a
    cl[...] = b
    plow[...] = b
    for k in range(STEPS):
        fext[k, INNER:INNER + SLAB, :] = fin[k].astype(F32)

    def square(k):
        @pl.loop(0, 4)
        def _(i):
            rows = pl.ds(pl.multiple_of(i * 128, 128), 128)
            xh, xl = pw[k - 1, rows, :], plow[rows, :]
            both = dot(jnp.concatenate([xh, xl], axis=0), pw[k - 1])
            ptmp[rows, :] = both[:128] + both[128:] + dot(xh, plow[...])

        high, low = split(ptmp[...])
        pw[k] = high
        plow[...] = low

    @pl.when(is_owner)
    def _():
        square(1)
        square(2)

    for load in loads[2:5]:
        load.wait()
    for copy in halos:
        copy.wait_recv()

    spread = din[...].astype(F32)
    half = 0.5 * vin[...].astype(F32)
    wext[0] = spread + half
    wext[1] = 1.0 - 2.0 * spread
    wext[2] = spread - half
    for side, at in ((0, 0), (1, INNER + SLAB)):
        packed = fhalo[side].astype(F32)
        for k in range(STEPS):
            if k < 4:
                rows = packed[8 * k:8 * k + 8]
            elif k < 7:
                rows = packed[8 * (6 - k):8 * (7 - k)]
                rows = pltpu.roll(rows, INNER - (7 - k) if side == 0 else 7 - k, 0)
            else:
                rows = jnp.zeros((INNER, NY), F32)
            fext[k, at:at + INNER, :] = rows

    @pl.when(first)
    def _():
        for copy in u_halos:
            copy.wait_recv()

    def advance(v, weights, forced):
        west, centre, east = weights
        rows = v.shape[0]
        mixed = centre * v + east * pltpu.roll(v, rows - 1, 0) + west * pltpu.roll(v, 1, 0)
        if forced is not None:
            mixed = mixed + forced
        return dot3(mixed, mh[...], ml[...])

    def weights64():
        return tuple(wext[i, 8:72, :] for i in range(3))

    def sweep(v, weights, forced):
        def turn(k, v):
            return advance(v, weights(), fext[k] if forced else None)
        return lax.fori_loop(0, STEPS, turn, v)

    def weights80():
        return tuple(wext[i] for i in range(3))

    def shift(src, dst, at):
        return [
            remote(src, dst.at[pl.ds(INNER, SLAB)], sh_send.at[at], sh_recv.at[at], p + 1, s),
            remote(src.at[pl.ds(0, INNER)], dst.at[pl.ds(INNER + SLAB, INNER)],
                   sh_send.at[at + 1], sh_recv.at[at + 1], p + 1, up),
            remote(src.at[pl.ds(SLAB - INNER, INNER)], dst.at[pl.ds(0, INNER)],
                   sh_send.at[at + 2], sh_recv.at[at + 2], p + 1, down),
        ]

    def start_shift(copies):
        @pl.when(p < NTM - 1)
        def _():
            for copy in copies:
                copy.start()

    def end_shift(copies, dst):
        @pl.when(p > 0)
        def _():
            for copy in copies:
                copy.wait_recv()

        @pl.when(first)
        def _():
            dst[...] = jnp.zeros_like(dst)

    begin = jnp.where(first, uin[...], jnp.zeros((64, NY), F32))
    bsend[...] = sweep(begin, weights64, True)[8:56]
    b_copies = shift(bsend, brecv, 0)
    start_shift(b_copies)

    @pl.when(is_owner)
    def _():
        square(3)
        square(4)

    end_shift(b_copies, brecv)
    dsend[...] = sweep(brecv[...], weights64, False)[8:56]
    d_copies = shift(dsend, drecv, 3)

    def forward(which, rows):
        for g in range(GROUPS):
            flat[pl.ds(g, SLAB, stride=GROUPS), :] = rows[:, g * LANES:(g + 1) * LANES]
        fwd_send[which] = flat[...].astype(BF16)
        mine = pl.ds(pl.multiple_of(p * TILE, TILE), TILE)
        for j in range(OWNERS):
            part = pl.ds(j * TILE, TILE)
            copy = remote(fwd_send.at[which, part], fwd_recv.at[which, mine],
                          fs_sem.at[which], fr_sem.at[which], owner_of(j), s)

            @pl.when(p != owner_of(j))
            def _():
                copy.start()

            @pl.when(p == owner_of(j))
            def _():
                fwd_recv[which, mine, :] = fwd_send[which, part, :]

    def forward_end(which):
        def wait(n):
            remote(fwd_send.at[which, pl.ds(0, n * TILE)], fwd_recv.at[which, pl.ds(0, n * TILE)],
                   fs_sem.at[which], fr_sem.at[which], p, up).wait_send()

        @pl.when(is_owner)
        def _():
            wait(OWNERS - 1)

        @pl.when(jnp.logical_not(is_owner))
        def _():
            wait(OWNERS)

    def scan(which, delay, result):
        count = (NTM - 1) * TILE
        remote(fwd_recv.at[which, pl.ds(0, count)], fwd_recv.at[which, pl.ds(0, count)],
               fs_sem.at[which], fr_sem.at[which], p, up).wait_recv()
        flat2[...] = fwd_recv[which].astype(F32)
        size = NTM * ROWS
        total = jnp.concatenate([flat2[pl.ds(g, size, stride=GROUPS), :] for g in range(GROUPS)], axis=1)
        row = lax.broadcasted_iota(jnp.int32, (size, NY), 0)

        def later(x, blocks):
            return jnp.where(row >= blocks * ROWS, pltpu.roll(x, blocks * ROWS, 0), 0.0)

        total = later(total, delay)
        for k in range(5):
            total = total + dot(later(total, 1 << k).astype(BF16), pw[k])
        for g in range(GROUPS):
            flat2[pl.ds(g, size, stride=GROUPS), :] = total[:, g * LANES:(g + 1) * LANES]
        result[...] = flat2[...].astype(result.dtype)

    def back(which, src, dst, edge, top, bottom):
        def copy(block, place, space):
            return remote(src.at[pl.ds(pl.multiple_of(block * TILE, TILE), TILE)],
                          dst.at[pl.ds(pl.multiple_of(place * TILE, TILE), TILE)],
                          bks_sem.at[which], bkr_sem.at[which], block, space)

        if edge:
            @pl.when(top)
            def _():
                @pl.loop(0, NTM)
                def _(i):
                    copy(i, edge + OWNERS + chunk, up).start()

            @pl.when(bottom)
            def _():
                @pl.loop(0, NTM)
                def _(i):
                    copy(i, chunk - (OWNERS - edge), down).start()

        @pl.loop(1, NTM)
        def _(i):
            copy(lax.rem(p + i, NTM), edge + chunk, s).start()

        at = pl.ds(pl.multiple_of((edge + chunk) * TILE, TILE), TILE)
        dst[at, :] = src[pl.ds(pl.multiple_of(p * TILE, TILE), TILE), :]

    def back_wait(which, dst, edge):
        def wait(n):
            part = dst.at[pl.ds(0, n * TILE)]
            remote(part, part, bks_sem.at[which], bkr_sem.at[which], p, up).wait_recv()

        @pl.when(is_owner)
        def _():
            wait(OWNERS + 2 * edge - 1)

        @pl.when(jnp.logical_not(is_owner))
        def _():
            wait(OWNERS + 2 * edge)

    def back_end(which, edge_which, src, on_edge):
        def wait(n, src, which):
            part = src.at[pl.ds(0, n * TILE)]
            remote(part, part, bks_sem.at[which], bkr_sem.at[which], p, up).wait_send()

        @pl.when(is_owner)
        def _():
            wait(NTM - 1, src, which)

        @pl.when(on_edge)
        def _():
            wait(NTM, edge_send if edge_which == 2 else src, edge_which)

    def back_edges(src, dst, top, bottom):
        def copy(block, place, space):
            return remote(src.at[pl.ds(pl.multiple_of(block * TILE, TILE), TILE)],
                          dst.at[pl.ds(pl.multiple_of(place * TILE, TILE), TILE)],
                          bks_sem.at[2], bkr_sem.at[2], block, space)

        @pl.when(top)
        def _():
            @pl.loop(0, NTM)
            def _(i):
                copy(i, 2 + chunk, up).start()

        @pl.when(bottom)
        def _():
            @pl.loop(0, NTM)
            def _(i):
                copy(i, chunk - (OWNERS - 2), down).start()

    forward(0, dsend[...])
    start_shift(d_copies)

    @pl.when(is_owner)
    def _():
        scan(0, 2, back1_send)
        back(0, back1_send, back1_recv, 4, top_owner, bottom_owner)

    back_wait(0, back1_recv, 4)
    flat3[...] = back1_recv[...].astype(F32)
    before = jnp.concatenate([flat3[pl.ds(g, 80, stride=GROUPS), :] for g in range(GROUPS)], axis=1)

    chold[...] = dot3(before[8:72], pw[0], cl[...])
    v = advance(before, weights80(), None)
    previous_w = lax.fori_loop(1, STEPS, lambda k, v: advance(v, weights80(), None), v)[8:72]
    whold[...] = previous_w
    residual = sweep(previous_w - chold[...], weights64, False)[8:56]
    forward(1, residual)
    out[7] = bsend[...] + dsend[...] + residual
    end_shift(d_copies, drecv)
    out[7] = out[7] + sweep(drecv[...] + chold[...], weights64, False)[8:56]
    drecv[...] = brecv[...] + drecv[...] + whold[...]

    @pl.when(is_owner)
    def _():
        scan(1, 1, back2_send)
        edge_send[...] = back2_send[...].astype(BF16)
        back_edges(edge_send, edge_recv, top2_owner, bottom2_owner)
        back(1, back2_send, back2_recv, 0, None, None)

    back_wait(1, back2_recv, 0)
    own = jnp.concatenate([back2_recv[pl.ds(g, SLAB, stride=GROUPS), :] for g in range(GROUPS)], axis=1)
    remote(edge_recv, edge_recv, bks_sem.at[2], bkr_sem.at[2], p, up).wait_recv()
    flat3[0:4 * TILE, :] = edge_recv[...].astype(F32)
    beside = jnp.concatenate([flat3[pl.ds(g, 16, stride=GROUPS), :] for g in range(GROUPS)], axis=1)
    correction = jnp.concatenate([beside[:8], own, beside[8:]], axis=0)
    v = jnp.where(first, uin[...], drecv[...] + correction)
    end = out[7] + dot3(own, pw[0], cl[...])
    v = advance(v, weights64(), fext[0])
    out[7] = end
    out[0] = v[8:56]

    def last(k, v):
        v = advance(v, weights64(), fext[k])
        out[k] = v[8:56]
        return v

    lax.fori_loop(1, STEPS - 1, last, v)

    for sent in halos:
        sent.wait_send()

    @pl.when(first)
    def _():
        for sent in u_halos:
            sent.wait_send()

    @pl.when(p < NTM - 1)
    def _():
        for sent in b_copies + d_copies:
            sent.wait_send()

    forward_end(0)
    forward_end(1)
    back_end(0, 0, back1_send, top_owner | bottom_owner)
    back_end(1, 2, back2_send, top2_owner | bottom2_owner)


def per_device(initial_state, velocity, diffusion, forcing, implicit, coarse_implicit):
    V = pltpu.VMEM
    DMA = pltpu.SemaphoreType.DMA
    square = (NY, NY)
    scratch = [
        V(square, F32), V(square, F32), V(square, BF16), V(square, BF16), V(square, BF16),
        V((5,) + square, BF16), V(square, BF16), V(square, F32),
        V((STEPS, SLAB, NY), BF16), V((80, NY), BF16), V((80, NY), BF16), V((64, NY), F32),
        V((2, 32, NY), BF16), V((2, 32, NY), BF16),
        V((3, 80, NY), F32), V((STEPS, 64, NY), F32),
        V((SLAB, NY), F32), V((64, NY), F32), V((SLAB, NY), F32), V((64, NY), F32),
        V((SLAB * GROUPS, LANES), F32), V((2, SLAB * GROUPS, LANES), BF16),
        V((2, NTM * TILE, LANES), BF16), V((NTM * TILE, LANES), F32),
        V((NTM * TILE, LANES), BF16), V((80 * GROUPS, LANES), BF16), V((80 * GROUPS, LANES), F32),
        V((NTM * TILE, LANES), F32), V((SLAB * GROUPS, LANES), F32),
        V((NTM * TILE, LANES), BF16), V((4 * TILE, LANES), BF16), V((64, NY), F32), V((64, NY), F32),
        DMA((6,)), DMA((6,)), DMA((6,)), DMA((2,)), DMA((2,)), DMA((6,)), DMA((6,)),
        DMA((2,)), DMA((2,)), DMA((3,)), DMA((3,)),
    ]
    return pl.pallas_call(
        kernel,
        out_shape=jax.ShapeDtypeStruct((STEPS, SLAB, NY), F32),
        in_specs=[pl.BlockSpec(memory_space=pl.ANY)] * 6,
        out_specs=pl.BlockSpec(memory_space=pltpu.VMEM),
        scratch_shapes=scratch,
        compiler_params=pltpu.CompilerParams(
            collective_id=0, has_side_effects=True, vmem_limit_bytes=40 * 2**20),
    )(*[pltpu.with_memory_space_constraint(x, pltpu.HBM)
        for x in (initial_state, velocity, diffusion, forcing, implicit, coarse_implicit)])


def solution(mesh):
    in_specs = (
        P("space", None),
        P("space", None),
        P("space", None),
        P("tm", "space", None),
        P(),
        P(),
    )
    return jax.shard_map(
        per_device, mesh=mesh, in_specs=in_specs, out_specs=P("tm", "space", None), check_vma=False
    )
```

```python
import functools

import jax
import jax.numpy as jnp
from jax import lax
from jax.experimental import pallas as pl
from jax.experimental.pallas import tpu as pltpu
from jax.sharding import PartitionSpec as P

F32, BF16 = jnp.float32, jnp.bfloat16
MESH = pl.DeviceIdType.MESH

STEPS = 8
NTM = 32
SLAB = 48
NY = 512
LANES = 128
GROUPS = NY // LANES
OWNERS = 12
ROWS = SLAB // OWNERS
TILE = ROWS * GROUPS
OUTER = 16
INNER = 8


OWNER_OF = (8, 10, 12, 14, 9, 13, 19, 23, 16, 18, 20, 22)


def owner_of(chunk):
    return OWNER_OF[chunk]


def split(x):
    high = x.astype(BF16)
    return high, (x - high.astype(F32)).astype(BF16)


def dot(a, b):
    return jnp.dot(a, b, preferred_element_type=F32)


def dot3(x, high, low):
    rows = x.shape[0]
    xh, xl = split(x)
    both = dot(jnp.concatenate([xh, xl], axis=0), high)
    return both[:rows] + both[rows:] + dot(xh, low)


def kernel(u0_hbm, vel_hbm, dif_hbm, forcing_hbm, imp_hbm, coarse_hbm, out,
           mv, cv, mh, ml, cl, pw, plow, ptmp, fin, vin, din, uin, fpack, fhalo,
           wext, fext, bsend, brecv, dsend, drecv, flat, fwd_send, fwd_recv, flat2,
           back1_send, back1_recv, flat3, back2_send, back2_recv, edge_send, edge_recv, edge_out, edge_in, chold, whold,
           in_sem, halo_send, halo_recv, u_send, u_recv, sh_send, sh_recv,
           fs_sem, fr_sem, bks_sem, bkr_sem):
    p = lax.axis_index("tm")
    s = lax.axis_index("space")
    nsp = lax.axis_size("space")
    up = lax.rem(s + nsp - 1, nsp)
    down = lax.rem(s + 1, nsp)
    first = p == 0
    chunk = jnp.int32(-1)
    for j in range(OWNERS):
        chunk = jnp.where(p == OWNER_OF[j], j, chunk)
    is_owner = chunk >= 0
    top_owner = is_owner & (chunk < 4)
    bottom_owner = is_owner & (chunk >= OWNERS - 4)
    top2_owner = is_owner & (chunk < 2)
    bottom2_owner = is_owner & (chunk >= OWNERS - 2)

    loads = [
        pltpu.make_async_copy(forcing_hbm, fin, in_sem.at[0]),
        pltpu.make_async_copy(imp_hbm, mv, in_sem.at[1]),
        pltpu.make_async_copy(vel_hbm, vin.at[pl.ds(OUTER, SLAB)], in_sem.at[2]),
        pltpu.make_async_copy(dif_hbm, din.at[pl.ds(OUTER, SLAB)], in_sem.at[3]),
        pltpu.make_async_copy(u0_hbm, uin.at[pl.ds(INNER, SLAB)], in_sem.at[4]),
        pltpu.make_async_copy(coarse_hbm, cv, in_sem.at[5]),
    ]
    for load in loads:
        load.start()

    barrier = pltpu.get_barrier_semaphore()

    def greet(tm, space):
        pl.semaphore_signal(barrier, inc=1, device_id=(tm, space), device_id_type=MESH)

    greet(p, up)
    greet(p, down)

    @pl.when(p > 0)
    def _():
        for other in (up, s, down):
            greet(p - 1, other)

    @pl.when(is_owner)
    def _():
        @pl.loop(1, NTM)
        def _(i):
            greet(lax.rem(p + i, NTM), s)

    total = 2 + OWNERS - jnp.where(is_owner, 1, 0) + jnp.where(p < NTM - 1, 3, 0)
    pl.semaphore_wait(barrier, total)

    def remote(src, dst, send, recv, tm, space):
        return pltpu.make_async_remote_copy(src_ref=src, dst_ref=dst, send_sem=send, recv_sem=recv,
                                            device_id=(tm, space), device_id_type=MESH)

    edge_low, edge_high = pl.ds(0, OUTER), pl.ds(OUTER + SLAB, OUTER)
    own_low, own_high = pl.ds(0, 16), pl.ds(SLAB - 16, 16)
    halos = [
        remote(fpack.at[0], fhalo.at[0], halo_send.at[0], halo_recv.at[0], p, down),
        remote(fpack.at[1], fhalo.at[1], halo_send.at[1], halo_recv.at[1], p, up),
        remote(vel_hbm.at[own_high], vin.at[edge_low], halo_send.at[2], halo_recv.at[2], p, down),
        remote(vel_hbm.at[own_low], vin.at[edge_high], halo_send.at[3], halo_recv.at[3], p, up),
        remote(dif_hbm.at[own_high], din.at[edge_low], halo_send.at[4], halo_recv.at[4], p, down),
        remote(dif_hbm.at[own_low], din.at[edge_high], halo_send.at[5], halo_recv.at[5], p, up),
    ]
    for copy in halos[2:]:
        copy.start()
    u_halos = [
        remote(u0_hbm.at[pl.ds(SLAB - INNER, INNER)], uin.at[pl.ds(0, INNER)], u_send.at[0], u_recv.at[0], p, down),
        remote(u0_hbm.at[pl.ds(0, INNER)], uin.at[pl.ds(INNER + SLAB, INNER)], u_send.at[1], u_recv.at[1], p, up),
    ]

    @pl.when(first)
    def _():
        for copy in u_halos:
            copy.start()

    loads[0].wait()
    sub = lax.broadcasted_iota(jnp.int32, (INNER, NY), 0)
    lower = [fin[k, SLAB - 16:SLAB, :].astype(F32)[8:] for k in range(7)]
    upper = [fin[k, 0:16, :].astype(F32)[:8] for k in range(7)]
    for side, rows in ((0, lower), (1, upper)):
        packed = []
        for k in range(4):
            if k == 3:
                packed.append(rows[3])
                continue
            count = k + 1
            if side == 0:
                moved = pltpu.roll(rows[6 - k], count, 0)
                packed.append(jnp.where(sub < count, moved, rows[k]))
            else:
                moved = pltpu.roll(rows[6 - k], INNER - count, 0)
                packed.append(jnp.where(sub >= INNER - count, moved, rows[k]))
        fpack[side] = jnp.concatenate(packed, axis=0).astype(BF16)

    for copy in halos[:2]:
        copy.start()

    loads[1].wait()
    a, b = split(mv[...])
    mh[...] = a
    ml[...] = b
    loads[5].wait()
    a, b = split(cv[...])
    pw[0] = a
    cl[...] = b
    plow[...] = b
    for k in range(STEPS):
        fext[k, INNER:INNER + SLAB, :] = fin[k].astype(F32)

    def square(k):
        @pl.loop(0, 4)
        def _(i):
            rows = pl.ds(pl.multiple_of(i * 128, 128), 128)
            xh, xl = pw[k - 1, rows, :], plow[rows, :]
            both = dot(jnp.concatenate([xh, xl], axis=0), pw[k - 1])
            ptmp[rows, :] = both[:128] + both[128:] + dot(xh, plow[...])

        high, low = split(ptmp[...])
        pw[k] = high
        plow[...] = low

    @pl.when(is_owner)
    def _():
        square(1)
        square(2)

    for load in loads[2:5]:
        load.wait()
    for copy in halos:
        copy.wait_recv()

    spread = din[...].astype(F32)
    half = 0.5 * vin[...].astype(F32)
    wext[0] = spread + half
    wext[1] = 1.0 - 2.0 * spread
    wext[2] = spread - half
    for side, at in ((0, 0), (1, INNER + SLAB)):
        packed = fhalo[side].astype(F32)
        for k in range(STEPS):
            if k < 4:
                rows = packed[8 * k:8 * k + 8]
            elif k < 7:
                rows = packed[8 * (6 - k):8 * (7 - k)]
                rows = pltpu.roll(rows, INNER - (7 - k) if side == 0 else 7 - k, 0)
            else:
                rows = jnp.zeros((INNER, NY), F32)
            fext[k, at:at + INNER, :] = rows

    @pl.when(first)
    def _():
        for copy in u_halos:
            copy.wait_recv()

    def advance(v, weights, forced):
        west, centre, east = weights
        rows = v.shape[0]
        mixed = centre * v + east * pltpu.roll(v, rows - 1, 0) + west * pltpu.roll(v, 1, 0)
        if forced is not None:
            mixed = mixed + forced
        return dot3(mixed, mh[...], ml[...])

    def weights64():
        return tuple(wext[i, 8:72, :] for i in range(3))

    def sweep(v, weights, forced):
        def turn(k, v):
            return advance(v, weights(), fext[k] if forced else None)
        return lax.fori_loop(0, STEPS, turn, v)

    def weights80():
        return tuple(wext[i] for i in range(3))

    def shift(src, dst, at):
        which = at // 3
        for side, start in ((0, 0), (1, SLAB - INNER)):
            rows = src[start:start + INNER, :]
            edge_out[which, side] = jnp.concatenate([rows[:, :NY // 2], rows[:, NY // 2:]], axis=0).astype(BF16)
        return [
            remote(src, dst.at[pl.ds(INNER, SLAB)], sh_send.at[at], sh_recv.at[at], p + 1, s),
            remote(edge_out.at[which, 0], edge_in.at[which, 1], sh_send.at[at + 1], sh_recv.at[at + 1], p + 1, up),
            remote(edge_out.at[which, 1], edge_in.at[which, 0], sh_send.at[at + 2], sh_recv.at[at + 2], p + 1, down),
        ]

    def start_shift(copies):
        @pl.when(p < NTM - 1)
        def _():
            for copy in copies:
                copy.start()

    def end_shift(copies, dst, which):
        @pl.when(p > 0)
        def _():
            for copy in copies:
                copy.wait_recv()
            for side, start in ((0, 0), (1, INNER + SLAB)):
                rows = edge_in[which, side].astype(F32)
                dst[start:start + INNER, :] = jnp.concatenate([rows[:INNER], rows[INNER:]], axis=1)

        @pl.when(first)
        def _():
            dst[...] = jnp.zeros_like(dst)

    begin = jnp.where(first, uin[...], jnp.zeros((64, NY), F32))
    bsend[...] = sweep(begin, weights64, True)[8:56]
    b_copies = shift(bsend, brecv, 0)
    start_shift(b_copies)

    @pl.when(is_owner)
    def _():
        square(3)
        square(4)

    end_shift(b_copies, brecv, 0)
    dsend[...] = sweep(brecv[...], weights64, False)[8:56]
    d_copies = shift(dsend, drecv, 3)

    def forward(which, rows):
        for g in range(GROUPS):
            flat[pl.ds(g, SLAB, stride=GROUPS), :] = rows[:, g * LANES:(g + 1) * LANES]
        fwd_send[which] = flat[...].astype(BF16)
        mine = pl.ds(pl.multiple_of(p * TILE, TILE), TILE)
        for j in range(OWNERS):
            part = pl.ds(j * TILE, TILE)
            copy = remote(fwd_send.at[which, part], fwd_recv.at[which, mine],
                          fs_sem.at[which], fr_sem.at[which], owner_of(j), s)

            @pl.when(p != owner_of(j))
            def _():
                copy.start()

            @pl.when(p == owner_of(j))
            def _():
                fwd_recv[which, mine, :] = fwd_send[which, part, :]

    def forward_end(which):
        def wait(n):
            remote(fwd_send.at[which, pl.ds(0, n * TILE)], fwd_recv.at[which, pl.ds(0, n * TILE)],
                   fs_sem.at[which], fr_sem.at[which], p, up).wait_send()

        @pl.when(is_owner)
        def _():
            wait(OWNERS - 1)

        @pl.when(jnp.logical_not(is_owner))
        def _():
            wait(OWNERS)

    def scan(which, delay, result):
        count = (NTM - 1) * TILE
        remote(fwd_recv.at[which, pl.ds(0, count)], fwd_recv.at[which, pl.ds(0, count)],
               fs_sem.at[which], fr_sem.at[which], p, up).wait_recv()
        flat2[...] = fwd_recv[which].astype(F32)
        size = NTM * ROWS
        total = jnp.concatenate([flat2[pl.ds(g, size, stride=GROUPS), :] for g in range(GROUPS)], axis=1)
        row = lax.broadcasted_iota(jnp.int32, (size, NY), 0)

        def later(x, blocks):
            return jnp.where(row >= blocks * ROWS, pltpu.roll(x, blocks * ROWS, 0), 0.0)

        total = later(total, delay)
        for k in range(5):
            total = total + dot(later(total, 1 << k).astype(BF16), pw[k])
        for g in range(GROUPS):
            flat2[pl.ds(g, size, stride=GROUPS), :] = total[:, g * LANES:(g + 1) * LANES]
        result[...] = flat2[...].astype(result.dtype)

    def back(which, src, dst, edge, top, bottom):
        def copy(block, place, space):
            return remote(src.at[pl.ds(pl.multiple_of(block * TILE, TILE), TILE)],
                          dst.at[pl.ds(pl.multiple_of(place * TILE, TILE), TILE)],
                          bks_sem.at[which], bkr_sem.at[which], block, space)

        if edge:
            @pl.when(top)
            def _():
                @pl.loop(0, NTM)
                def _(i):
                    copy(i, edge + OWNERS + chunk, up).start()

            @pl.when(bottom)
            def _():
                @pl.loop(0, NTM)
                def _(i):
                    copy(i, chunk - (OWNERS - edge), down).start()

        @pl.loop(1, NTM)
        def _(i):
            copy(lax.rem(p + i, NTM), edge + chunk, s).start()

        at = pl.ds(pl.multiple_of((edge + chunk) * TILE, TILE), TILE)
        dst[at, :] = src[pl.ds(pl.multiple_of(p * TILE, TILE), TILE), :]

    def back_wait(which, dst, edge):
        def wait(n):
            part = dst.at[pl.ds(0, n * TILE)]
            remote(part, part, bks_sem.at[which], bkr_sem.at[which], p, up).wait_recv()

        @pl.when(is_owner)
        def _():
            wait(OWNERS + 2 * edge - 1)

        @pl.when(jnp.logical_not(is_owner))
        def _():
            wait(OWNERS + 2 * edge)

    def back_end(which, edge_which, src, on_edge):
        def wait(n, src, which):
            part = src.at[pl.ds(0, n * TILE)]
            remote(part, part, bks_sem.at[which], bkr_sem.at[which], p, up).wait_send()

        @pl.when(is_owner)
        def _():
            wait(NTM - 1, src, which)

        @pl.when(on_edge)
        def _():
            wait(NTM, edge_send if edge_which == 2 else src, edge_which)

    def back_edges(src, dst, top, bottom):
        def copy(block, place, space):
            return remote(src.at[pl.ds(pl.multiple_of(block * TILE, TILE), TILE)],
                          dst.at[pl.ds(pl.multiple_of(place * TILE, TILE), TILE)],
                          bks_sem.at[2], bkr_sem.at[2], block, space)

        @pl.when(top)
        def _():
            @pl.loop(0, NTM)
            def _(i):
                copy(i, 2 + chunk, up).start()

        @pl.when(bottom)
        def _():
            @pl.loop(0, NTM)
            def _(i):
                copy(i, chunk - (OWNERS - 2), down).start()

    forward(0, dsend[...])
    start_shift(d_copies)

    @pl.when(is_owner)
    def _():
        scan(0, 2, back1_send)
        back(0, back1_send, back1_recv, 4, top_owner, bottom_owner)

    back_wait(0, back1_recv, 4)
    flat3[...] = back1_recv[...].astype(F32)
    before = jnp.concatenate([flat3[pl.ds(g, 80, stride=GROUPS), :] for g in range(GROUPS)], axis=1)

    chold[...] = dot3(before[8:72], pw[0], cl[...])
    v = advance(before, weights80(), None)
    previous_w = lax.fori_loop(1, STEPS, lambda k, v: advance(v, weights80(), None), v)[8:72]
    whold[...] = previous_w
    residual = sweep(previous_w - chold[...], weights64, False)[8:56]
    forward(1, residual)
    out[7] = bsend[...] + dsend[...] + residual
    end_shift(d_copies, drecv, 1)
    out[7] = out[7] + sweep(drecv[...] + chold[...], weights64, False)[8:56]
    drecv[...] = brecv[...] + drecv[...] + whold[...]

    @pl.when(is_owner)
    def _():
        scan(1, 1, back2_send)
        edge_send[...] = back2_send[...].astype(BF16)
        back_edges(edge_send, edge_recv, top2_owner, bottom2_owner)
        back(1, back2_send, back2_recv, 0, None, None)

    back_wait(1, back2_recv, 0)
    own = jnp.concatenate([back2_recv[pl.ds(g, SLAB, stride=GROUPS), :] for g in range(GROUPS)], axis=1)
    remote(edge_recv, edge_recv, bks_sem.at[2], bkr_sem.at[2], p, up).wait_recv()
    flat3[0:4 * TILE, :] = edge_recv[...].astype(F32)
    beside = jnp.concatenate([flat3[pl.ds(g, 16, stride=GROUPS), :] for g in range(GROUPS)], axis=1)
    correction = jnp.concatenate([beside[:8], own, beside[8:]], axis=0)
    v = jnp.where(first, uin[...], drecv[...] + correction)
    end = out[7] + dot3(own, pw[0], cl[...])
    v = advance(v, weights64(), fext[0])
    out[7] = end
    out[0] = v[8:56]

    def last(k, v):
        v = advance(v, weights64(), fext[k])
        out[k] = v[8:56]
        return v

    lax.fori_loop(1, STEPS - 1, last, v)

    for sent in halos:
        sent.wait_send()

    @pl.when(first)
    def _():
        for sent in u_halos:
            sent.wait_send()

    @pl.when(p < NTM - 1)
    def _():
        for sent in b_copies + d_copies:
            sent.wait_send()

    forward_end(0)
    forward_end(1)
    back_end(0, 0, back1_send, top_owner | bottom_owner)
    back_end(1, 2, back2_send, top2_owner | bottom2_owner)


def per_device(initial_state, velocity, diffusion, forcing, implicit, coarse_implicit):
    V = pltpu.VMEM
    DMA = pltpu.SemaphoreType.DMA
    square = (NY, NY)
    scratch = [
        V(square, F32), V(square, F32), V(square, BF16), V(square, BF16), V(square, BF16),
        V((5,) + square, BF16), V(square, BF16), V(square, F32),
        V((STEPS, SLAB, NY), BF16), V((80, NY), BF16), V((80, NY), BF16), V((64, NY), F32),
        V((2, 32, NY), BF16), V((2, 32, NY), BF16),
        V((3, 80, NY), F32), V((STEPS, 64, NY), F32),
        V((SLAB, NY), F32), V((64, NY), F32), V((SLAB, NY), F32), V((64, NY), F32),
        V((SLAB * GROUPS, LANES), F32), V((2, SLAB * GROUPS, LANES), BF16),
        V((2, NTM * TILE, LANES), BF16), V((NTM * TILE, LANES), F32),
        V((NTM * TILE, LANES), BF16), V((80 * GROUPS, LANES), BF16), V((80 * GROUPS, LANES), F32),
        V((NTM * TILE, LANES), F32), V((SLAB * GROUPS, LANES), F32),
        V((NTM * TILE, LANES), BF16), V((4 * TILE, LANES), BF16),
        V((2, 2, 16, NY // 2), BF16), V((2, 2, 16, NY // 2), BF16), V((64, NY), F32), V((64, NY), F32),
        DMA((6,)), DMA((6,)), DMA((6,)), DMA((2,)), DMA((2,)), DMA((6,)), DMA((6,)),
        DMA((2,)), DMA((2,)), DMA((3,)), DMA((3,)),
    ]
    return pl.pallas_call(
        kernel,
        out_shape=jax.ShapeDtypeStruct((STEPS, SLAB, NY), F32),
        in_specs=[pl.BlockSpec(memory_space=pl.ANY)] * 6,
        out_specs=pl.BlockSpec(memory_space=pltpu.VMEM),
        scratch_shapes=scratch,
        compiler_params=pltpu.CompilerParams(
            collective_id=0, has_side_effects=True, vmem_limit_bytes=40 * 2**20),
    )(*[pltpu.with_memory_space_constraint(x, pltpu.HBM)
        for x in (initial_state, velocity, diffusion, forcing, implicit, coarse_implicit)])


def solution(mesh):
    in_specs = (
        P("space", None),
        P("space", None),
        P("space", None),
        P("tm", "space", None),
        P(),
        P(),
    )
    return jax.shard_map(
        per_device, mesh=mesh, in_specs=in_specs, out_specs=P("tm", "space", None), check_vma=False
    )
```
